128 devices in a mesh: pt: 16 (over y, x), ct: 8 (over z, core).
Axes of the slice: x: 4, y: 4, z: 4, core: 2. Of those that a mesh axis runs over, the one named last changes fastest.
Arguments:
- points: float32 [32768, 128], P('pt'), may hold values from -8 to 8, as said below
- centroids: float32 [16384, 128], P('ct'), may hold values from -4 to 4, as said below
- cotangent: float32 [32768, 128], P('pt'), may hold values from -6 to 6
Outputs:
- point_grad: float32 [32768, 128], P(('pt', 'ct'))
- centroid_grad_out: float32 [16384, 128], P('ct')
The draws below stay inside these ranges and needn't reach their ends.
Inputs may be any that keep to these rules, and one draw needn't show every extreme that they name: `points`: embedding entries of order one. `centroids`: centroid entries of order one.
All inputs are finite; a program needn't handle non-finite values.
Results may differ from the reference program's by a relative error of at most 0.0003.
Values sent between devices are 32-bit elements; how exact they have to be, the bound alone decides.
No kernel may reach another device: no remote copies, remote signals or barrier semaphores. Data moves between devices by JAX's collectives and lax.ppermute only.
A program may use at most 128 MiB of HBM per device.

```python
import math
import jax
import jax.numpy as jnp
from jax import lax

D = 128
BLOCK = 512
NP = 32768
NC = 16384


def centroid_table(key):
    normal_part = jnp.clip(jax.random.normal(key, (NC, D), jnp.float32), -4.0, 4.0)
    return normal_part


def draw_centroids(key, part):
    return centroid_table(key)


def draw_points(key, part):
    own = jax.random.fold_in(key, 11)
    spread = jnp.exp(jax.random.uniform(jax.random.fold_in(own, 1), (NP, 1), jnp.float32, -0.69, 0.69))
    return jnp.clip(jax.random.normal(own, (NP, D), jnp.float32), -4.0, 4.0) * spread


def steps_of(key, dims, shards, low, top_value):
    loudness = 1.0
    for position, shards_of in shards:
        draws = jax.random.uniform(jax.random.fold_in(jax.random.fold_in(key, 6), position), (shards_of,), jnp.float32, low / len(shards), top_value / len(shards))
        loudness = loudness * jnp.repeat(jnp.exp(draws), dims[position] // shards_of).reshape((-1,) + (1,) * (len(dims) - 1 - position))
    return loudness


def centred(own_key, dims, deviation, reach, split=(), dtype=jnp.bfloat16):
    drawn = jax.random.normal(own_key, dims, jnp.float32) * deviation
    if len(split) > 0:
        drawn = steps_of(own_key, dims, split, -0.22, 0.18) * drawn
    return jnp.clip(drawn, min=-reach, max=reach).astype(dtype)


def setup_inputs(seed: int = 0) -> dict:
    splits = jax.random.split(jax.random.key(seed), 4)
    points = draw_points(jax.random.fold_in(splits[3], 71), 0)
    centroids = draw_centroids(jax.random.fold_in(splits[3], 71), 0)
    cotangent = centred(splits[2], (NP, D), 1.0, 6.0, ((0, 16),), jnp.float32)
    return {"points": points, "centroids": centroids, "cotangent": cotangent}


def logits(block_rows, cent, scale):
    return scale * jnp.dot(block_rows, cent.T, precision=lax.Precision.HIGHEST, preferred_element_type=jnp.float32)

def reference(points, centroids, cotangent):
    n_rows, width = points.shape
    n_cols = centroids.shape[0]
    scale = 3.0 / math.sqrt(width)
    ratio_log = math.log(n_rows / n_cols)
    ratio = n_cols / n_rows
    blocks = points.reshape(-1, BLOCK, width)
    cots = cotangent.reshape(-1, BLOCK, width)

    def row_lse(col_shift):

        def one(block_rows):
            return jax.nn.logsumexp(logits(block_rows, centroids, scale) + col_shift[None, :], axis=1)
        return lax.map(one, blocks).reshape(-1)

    def col_lse(row_shift):

        def step(carry, item):
            peak, total = carry
            block_rows, shift = item
            shifted = logits(block_rows, centroids, scale) + shift[:, None]
            newpeak = jnp.maximum(peak, lax.optimization_barrier(jnp.max(shifted, axis=0)))
            total = total * jnp.exp(peak - newpeak) + lax.optimization_barrier(jnp.sum(jnp.exp(shifted - newpeak[None, :]), axis=0))
            return ((newpeak, total), None)
        init = (jnp.full((n_cols,), -1e+30, jnp.float32), jnp.zeros((n_cols,), jnp.float32))
        (peak, total), _ = lax.scan(step, init, (blocks, row_shift.reshape(-1, BLOCK)))
        return peak + jnp.log(total)
    zero_cols = jnp.zeros((n_cols,), jnp.float32)
    f1 = -row_lse(zero_cols)
    g1 = ratio_log - col_lse(f1)
    f2 = -row_lse(g1)
    g2 = ratio_log - col_lse(f2)
    f1b = f1.reshape(-1, BLOCK)
    f2b = f2.reshape(-1, BLOCK)

    def edge_step(carry, item):
        col_edge, direct = carry
        block_rows, cot, shift = item
        plan = jnp.exp(logits(block_rows, centroids, scale) + shift[:, None] + g2[None, :])
        wmat = jnp.dot(cot, centroids.T, precision=lax.Precision.HIGHEST, preferred_element_type=jnp.float32)
        edge = plan * wmat
        direct = direct + jnp.einsum('ij,id->jd', plan, cot, precision=lax.Precision.HIGHEST)
        return ((col_edge + lax.optimization_barrier(jnp.sum(edge, axis=0)), direct), lax.optimization_barrier(jnp.sum(edge, axis=1)))
    init = (jnp.zeros((n_cols,), jnp.float32), jnp.zeros((n_cols, width), jnp.float32))
    (dg2, direct), row_edge = lax.scan(edge_step, init, (blocks, cots, f2b))
    row_edge = row_edge.reshape(-1)

    def weighted(item):
        block_rows, shift = item
        plan = jnp.exp(logits(block_rows, centroids, scale) + shift[:, None] + g2[None, :])
        return lax.optimization_barrier(jnp.sum(plan * dg2[None, :], axis=1))
    df2 = row_edge - ratio * lax.map(weighted, (blocks, f2b)).reshape(-1)
    df2b = df2.reshape(-1, BLOCK)

    def col_step(carry, item):
        block_rows, shift, back = item
        second = jnp.exp(logits(block_rows, centroids, scale) + g1[None, :] + shift[:, None])
        return (carry - lax.optimization_barrier(jnp.sum(second * back[:, None], axis=0)), None)
    dg1, _ = lax.scan(col_step, jnp.zeros((n_cols,), jnp.float32), (blocks, f2b, df2b))

    def row_back(item):
        block_rows, shift = item
        first = jnp.exp(logits(block_rows, centroids, scale) + shift[:, None] + g1[None, :] - ratio_log)
        return -lax.optimization_barrier(jnp.sum(first * dg1[None, :], axis=1))
    df1b = lax.map(row_back, (blocks, f1b))

    def grad_step(carry, item):
        block_rows, cot, s1, s2, b2, b1 = item
        zval = logits(block_rows, centroids, scale)
        plan = jnp.exp(zval + s2[:, None] + g2[None, :])
        wmat = jnp.dot(cot, centroids.T, precision=lax.Precision.HIGHEST, preferred_element_type=jnp.float32)
        dz = plan * wmat - ratio * plan * dg2[None, :]
        dz = dz - jnp.exp(zval + g1[None, :] + s2[:, None]) * b2[:, None]
        dz = dz - jnp.exp(zval + s1[:, None] + g1[None, :] - ratio_log) * dg1[None, :]
        dz = dz - jnp.exp(zval + s1[:, None]) * b1[:, None]
        pgrad = scale * jnp.dot(dz, centroids, precision=lax.Precision.HIGHEST, preferred_element_type=jnp.float32)
        carry = carry + scale * jnp.einsum('ij,id->jd', dz, block_rows, precision=lax.Precision.HIGHEST)
        return (carry, pgrad)
    rest, pgrads = lax.scan(grad_step, jnp.zeros((n_cols, width), jnp.float32), (blocks, cots, f1b, f2b, df2b, df1b))
    return (pgrads.reshape(n_rows, width), direct + rest)
```

```python
import functools
import math

import jax
import jax.numpy as jnp
from jax import lax
from jax.experimental import pallas as pl
from jax.experimental.pallas import tpu as pltpu
from jax.sharding import PartitionSpec as P

L = 128
F32 = jnp.float32
BF16 = jnp.bfloat16
VMEM_LIMIT = 20 * 1024 * 1024


def split(x):
    high = x.astype(BF16)
    return high, (x - high.astype(F32)).astype(BF16)


def spread(vec_ref, index):
    return jnp.broadcast_to(vec_ref[pl.ds(index, 1), :], (L, L)).T


def fold_rows(tile):
    return jnp.sum(tile.T, axis=0, keepdims=True)


def fold_sub(tile, op):
    return op(tile.reshape(L // 8, 8, L), axis=0)


def cols_of(c):
    return slice(c * L, (c + 1) * L)


def rows_of(r):
    return pl.ds(pl.multiple_of(r * L, L), L)


def send(out_ref, lead, value):
    for n in range(out_ref.shape[0]):
        out_ref[(n,) + lead] = value


def copies(out_ref):
    for n in range(1, out_ref.shape[0]):
        out_ref[n] = out_ref[0]


def product(left_ref, right_ref, out_ref, a_ref, b_ref, scale):
    high, low = split(left_ref[...] * scale)
    for k, part in enumerate((high, high, low, low)):
        a_ref[:, cols_of(k)] = part
    high, low = split(right_ref[...])
    for k, part in enumerate((high, low, high, low)):
        b_ref[:, cols_of(k)] = part
    rows, cols = out_ref.shape
    tile = min(256, cols)
    chunk = min(512, rows)

    def body(step, carry):
        c = step // (rows // chunk)
        r = step % (rows // chunk)
        rs = pl.ds(pl.multiple_of(r * chunk, chunk), chunk)
        cs = pl.ds(pl.multiple_of(c * tile, tile), tile)
        out_ref[rs, cs] = lax.dot_general(
            a_ref[rs, :], b_ref[cs, :], (((1,), (1,)), ((), ())), preferred_element_type=F32
        )
        return carry

    lax.fori_loop(0, (cols // tile) * (rows // chunk), body, 0)


def scores_kernel(scale, p_ref, c_ref, z_ref, stat_ref, a_ref, b_ref):
    product(p_ref, c_ref, z_ref, a_ref, b_ref, scale)
    nr, nc = z_ref.shape[0] // L, z_ref.shape[1] // L

    def body(r, carry):
        rs = rows_of(r)
        top = z_ref[rs, cols_of(0)]
        for c in range(1, nc):
            top = jnp.maximum(top, z_ref[rs, cols_of(c)])
        peak = jnp.max(top.T, axis=0, keepdims=True)
        wide = jnp.broadcast_to(peak, (L, L)).T
        total = jnp.zeros((L, L), F32)
        for c in range(nc):
            total = total + jnp.exp(z_ref[rs, cols_of(c)] - wide)
        stat_ref[0, 0, pl.ds(r, 1), :] = peak
        stat_ref[0, 1, pl.ds(r, 1), :] = fold_rows(total)
        return carry

    lax.fori_loop(0, nr, body, 0)
    copies(stat_ref)


def weights_kernel(cot_ref, c_ref, w_ref, a_ref, b_ref):
    product(cot_ref, c_ref, w_ref, a_ref, b_ref, 1.0)


def merged(stat_ref):
    peak = stat_ref[0, 0]
    for n in range(1, stat_ref.shape[0]):
        peak = jnp.maximum(peak, stat_ref[n, 0])
    total = jnp.zeros_like(peak)
    for n in range(stat_ref.shape[0]):
        total = total + stat_ref[n, 1] * jnp.exp(stat_ref[n, 0] - peak)
    return peak + jnp.log(total)


def summed(ref, *lead):
    total = ref[(0,) + lead]
    for n in range(1, ref.shape[0]):
        total = total + ref[(n,) + lead]
    return total


def cols_kernel(z_ref, rowstat_ref, stat_ref, f1_ref, peak_ref, total_ref):
    nr, nc = z_ref.shape[0] // L, z_ref.shape[1] // L
    f1_ref[...] = -merged(rowstat_ref)
    peak_ref[...] = jnp.full_like(peak_ref, -jnp.inf)
    total_ref[...] = jnp.zeros_like(total_ref)

    def body(r, carry):
        rs = rows_of(r)
        shift = spread(f1_ref, r)
        for c in range(nc):
            cs = cols_of(c)
            shifted = z_ref[rs, cs] + shift
            old = peak_ref[:, cs]
            new = jnp.maximum(old, fold_sub(shifted, jnp.max))
            terms = jnp.exp(shifted.reshape(L // 8, 8, L) - new[None])
            total_ref[:, cs] = total_ref[:, cs] * jnp.exp(old - new) + jnp.sum(terms, axis=0)
            peak_ref[:, cs] = new
        return carry

    lax.fori_loop(0, nr, body, 0)
    for c in range(nc):
        cs = cols_of(c)
        peak = jnp.max(peak_ref[:, cs], axis=0, keepdims=True)
        total = jnp.sum(total_ref[:, cs] * jnp.exp(peak_ref[:, cs] - peak), axis=0, keepdims=True)
        stat_ref[0, 0, c : c + 1, :] = peak
        stat_ref[0, 1, c : c + 1, :] = total
    copies(stat_ref)


def plan_kernel(z_ref, colstat_ref, f1_ref, b_ref, sum_ref, s_ref, shift_ref):
    nr, nc = z_ref.shape[0] // L, z_ref.shape[1] // L
    lse = merged(colstat_ref)
    shift_ref[...] = -lse
    s_ref[...] = jnp.exp(lse)

    def body(r, carry):
        rs = rows_of(r)
        shift = spread(f1_ref, r)
        total = jnp.zeros((L, L), F32)
        for c in range(nc):
            cs = cols_of(c)
            value = jnp.exp((z_ref[rs, cs] + shift) + shift_ref[c : c + 1, :])
            b_ref[rs, cs] = value
            total = total + value
        sum_ref[0, pl.ds(r, 1), :] = fold_rows(total)
        return carry

    lax.fori_loop(0, nr, body, 0)
    copies(sum_ref)


def edges_kernel(b_ref, w_ref, rowsum_ref, stat_ref, ib_ref, one_ref, two_ref):
    nr, nc = b_ref.shape[0] // L, b_ref.shape[1] // L
    ib_ref[...] = 1.0 / summed(rowsum_ref)
    one_ref[...] = jnp.zeros_like(one_ref)
    two_ref[...] = jnp.zeros_like(two_ref)

    def body(r, carry):
        rs = rows_of(r)
        inv = spread(ib_ref, r)
        for c in range(nc):
            cs = cols_of(c)
            value = b_ref[rs, cs] * inv
            one_ref[:, cs] += fold_sub(value, jnp.sum)
            two_ref[:, cs] += fold_sub(value * w_ref[rs, cs], jnp.sum)
        return carry

    lax.fori_loop(0, nr, body, 0)
    for c in range(nc):
        cs = cols_of(c)
        stat_ref[0, 0, c : c + 1, :] = jnp.sum(one_ref[:, cs], axis=0, keepdims=True)
        stat_ref[0, 1, c : c + 1, :] = jnp.sum(two_ref[:, cs], axis=0, keepdims=True)
    copies(stat_ref)


def rowback_kernel(share, ratio, b_ref, w_ref, colsum_ref, g_ref, sum_ref, q_ref, h_ref):
    nr, nc = b_ref.shape[0] // L, b_ref.shape[1] // L
    q = share / summed(colsum_ref, 0)
    q_ref[...] = q
    h_ref[...] = ratio * (q * summed(colsum_ref, 1))

    def body(r, carry):
        rs = rows_of(r)
        total = jnp.zeros((L, L), F32)
        for c in range(nc):
            cs = cols_of(c)
            value = (b_ref[rs, cs] * q_ref[c : c + 1, :]) * (w_ref[rs, cs] - h_ref[c : c + 1, :])
            g_ref[rs, cs] = value
            total = total + value
        sum_ref[0, pl.ds(r, 1), :] = fold_rows(total)
        return carry

    lax.fori_loop(0, nr, body, 0)
    copies(sum_ref)


def colback_kernel(b_ref, rowsum_ref, ib_ref, sum_ref, y_ref, acc_ref):
    nr, nc = b_ref.shape[0] // L, b_ref.shape[1] // L
    y_ref[...] = (summed(rowsum_ref) * ib_ref[...]) * ib_ref[...]
    acc_ref[...] = jnp.zeros_like(acc_ref)

    def body(r, carry):
        rs = rows_of(r)
        y = spread(y_ref, r)
        for c in range(nc):
            cs = cols_of(c)
            acc_ref[:, cs] += fold_sub(b_ref[rs, cs] * y, jnp.sum)
        return carry

    lax.fori_loop(0, nr, body, 0)
    for c in range(nc):
        sum_ref[0, c : c + 1, :] = -jnp.sum(acc_ref[:, cols_of(c)], axis=0, keepdims=True)
    copies(sum_ref)


def lastrow_kernel(b_ref, colsum_ref, sum_ref, d_ref):
    nr, nc = b_ref.shape[0] // L, b_ref.shape[1] // L
    d_ref[...] = summed(colsum_ref)

    def body(r, carry):
        rs = rows_of(r)
        total = jnp.zeros((L, L), F32)
        for c in range(nc):
            total = total + b_ref[rs, cols_of(c)] * d_ref[c : c + 1, :]
        sum_ref[0, pl.ds(r, 1), :] = -fold_rows(total)
        return carry

    lax.fori_loop(0, nr, body, 0)
    copies(sum_ref)


def grads_kernel(
    scale, b_ref, g_ref, rowsum_ref, d_ref, y_ref, ib_ref, s_ref, q_ref, p_ref, c_ref, cot_ref,
    pg_ref, cg_ref, f_ref, pt_ref, ct_ref, cc_ref, dz_ref, bb_ref, one_ref, two_ref
):
    rows, cols = b_ref.shape
    nr, nc = rows // L, cols // L
    f_ref[...] = summed(rowsum_ref)
    high, low = split(c_ref[...] * scale)
    cc_ref[:, :L] = high
    cc_ref[:, L:] = low
    for r in range(nr):
        rs = slice(r * L, (r + 1) * L)
        high, low = split((p_ref[rs, :] * scale).T)
        pt_ref[:L, rs] = high
        pt_ref[L:, rs] = low
        high, low = split(cot_ref[rs, :].T * ib_ref[r : r + 1, :])
        ct_ref[:L, rs] = high
        ct_ref[L:, rs] = low
    one_ref[...] = jnp.zeros_like(one_ref)
    two_ref[...] = jnp.zeros_like(two_ref)
    chunk = min(256, rows)
    part = min(512, cols)

    def body(k, carry):
        for sub in range(chunk // L):
            r = k * (chunk // L) + sub
            rs = rows_of(r)
            inv, y, f = spread(ib_ref, r), spread(y_ref, r), spread(f_ref, r)
            here = slice(sub * L, (sub + 1) * L)
            there = slice(chunk + sub * L, chunk + (sub + 1) * L)
            for c in range(nc):
                cs = cols_of(c)
                base = b_ref[rs, cs]
                factor = (y + d_ref[c : c + 1, :]) + s_ref[c : c + 1, :] * f
                high, low = split(g_ref[rs, cs] * inv - base * factor)
                dz_ref[here, cs] = high
                dz_ref[there, cs] = low
                high, low = split(base)
                bb_ref[here, cs] = high
                bb_ref[there, cs] = low
        ks = pl.ds(pl.multiple_of(k * chunk, chunk), chunk)
        both = jnp.dot(dz_ref[...], cc_ref[...], preferred_element_type=F32)
        both = both[:, :L] + both[:, L:]
        pg_ref[ks, :] = both[:chunk] + both[chunk:]
        for n in range(cols // part):
            ns = slice(n * part, (n + 1) * part)
            for left, right, acc in ((pt_ref, dz_ref, one_ref), (ct_ref, bb_ref, two_ref)):
                lhs = left[:, ks]
                acc[:, ns] += jnp.dot(lhs, right[:chunk, ns], preferred_element_type=F32) + jnp.dot(
                    lhs, right[chunk:, ns], preferred_element_type=F32
                )
        return carry

    lax.fori_loop(0, rows // chunk, body, 0)
    for c in range(nc):
        cs = cols_of(c)
        plan = (two_ref[:L, cs] + two_ref[L:, cs]) * q_ref[c : c + 1, :]
        cg_ref[cs, :] = ((one_ref[:L, cs] + one_ref[L:, cs]) + plan).T


def call(kernel, name, outs, scratch, args, aliases=None, flops=0):
    big = lambda a: a.ndim == 2 and a.shape[0] >= 256 and a.shape[1] >= 256
    shapes = [
        pltpu.VMEM(o, F32) if len(o) == 2 and min(o) >= 256 else jax.ShapeDtypeStruct(o, F32)
        for o in outs
    ]
    args = [pltpu.with_memory_space_constraint(a, pltpu.VMEM) if big(a) else a for a in args]
    whole = pl.BlockSpec(memory_space=pltpu.VMEM)
    return pl.pallas_call(
        kernel,
        name=name,
        out_shape=shapes,
        in_specs=[whole] * len(args),
        out_specs=[whole] * len(outs),
        scratch_shapes=[pltpu.VMEM(s, t) for s, t in scratch],
        input_output_aliases=aliases or {},
        compiler_params=pltpu.CompilerParams(vmem_limit_bytes=VMEM_LIMIT),
        cost_estimate=pl.CostEstimate(flops=flops, bytes_accessed=1 << 20, transcendentals=0),
    )(*args)


def per_device(points, centroids, cotangent):
    rows, width = points.shape
    cols = centroids.shape[0]
    npt, nct = lax.axis_size("pt"), lax.axis_size("ct")
    share = (rows * npt) / (cols * nct)
    ratio = (cols * nct) / (rows * npt)
    scale = 3.0 / math.sqrt(width)
    nr, nc = rows // L, cols // L

    def over(axis, value):
        return lax.all_to_all(value, axis, 0, 0, tiled=True)

    big = (rows, cols)
    rvec, cvec = (nr, L), (nc, L)
    tall = [((rows, 4 * L), BF16), ((cols, 4 * L), BF16)]
    strip = ((8, cols), F32)
    z, stat = call(
        functools.partial(scores_kernel, scale), "scores", [big, (nct, 2) + rvec], tall,
        [points, centroids], flops=8 * rows * cols * L,
    )
    stat = over("ct", stat)
    (w,) = call(weights_kernel, "weights", [big], tall, [cotangent, centroids], flops=8 * rows * cols * L)
    stat, f1 = call(cols_kernel, "cols", [(npt, 2) + cvec, rvec], [strip, strip], [z, stat])
    stat = over("pt", stat)
    b, sums, s = call(
        plan_kernel, "plan", [big, (nct,) + rvec, cvec], [(cvec, F32)], [z, stat, f1], {0: 0}
    )
    sums = over("ct", sums)
    stat, ib = call(edges_kernel, "edges", [(npt, 2) + cvec, rvec], [strip, strip], [b, w, sums])
    stat = over("pt", stat)
    g, sums, q = call(
        functools.partial(rowback_kernel, share, ratio), "rowback",
        [big, (nct,) + rvec, cvec], [(cvec, F32)], [b, w, stat], {1: 0},
    )
    sums = over("ct", sums)
    sums, y = call(colback_kernel, "colback", [(npt,) + cvec, rvec], [strip], [b, sums, ib])
    sums = over("pt", sums)
    sums, d = call(lastrow_kernel, "lastrow", [(nct,) + rvec, cvec], [], [b, sums])
    sums = over("ct", sums)
    chunk = min(256, rows)
    pg, cg = call(
        functools.partial(grads_kernel, scale), "grads", [(rows, width), (cols, width)],
        [
            (rvec, F32), ((2 * L, rows), BF16), ((2 * L, rows), BF16), ((cols, 2 * L), BF16),
            ((2 * chunk, cols), BF16), ((2 * chunk, cols), BF16),
            ((2 * L, cols), F32), ((2 * L, cols), F32),
        ],
        [b, g, sums, d, y, ib, s, q, points, centroids, cotangent],
        flops=24 * rows * cols * L,
    )
    cg = over("pt", cg.reshape(npt, cols // npt, width))
    pg = over("ct", pg.reshape(nct, rows // nct, width))
    cg = jnp.sum(cg, axis=0)
    point_grad = jnp.sum(pg, axis=0)
    cg = over("pt", jnp.broadcast_to(cg[None], (npt, cols // npt, width)))
    return (point_grad, cg.reshape(cols, width))


def solution(mesh):
    return jax.shard_map(
        per_device,
        mesh=mesh,
        in_specs=(P("pt", None), P("ct", None), P("pt", None)),
        out_specs=(P(("pt", "ct"), None), P("ct", None)),
        check_vma=False,
    )
```

```python
import functools
import itertools
import math

import jax
import jax.numpy as jnp
from jax import lax
from jax.experimental import pallas as pl
from jax.experimental.pallas import tpu as pltpu
from jax.sharding import PartitionSpec as P

L = 128
F32 = jnp.float32
BF16 = jnp.bfloat16
ROW_UNROLL = 16
PLAN_UNROLL = 2
CHUNK = 256


def split(x):
    high = x.astype(BF16)
    return high, (x - high.astype(F32)).astype(BF16)


def spread(vec_ref, index):
    return jnp.broadcast_to(vec_ref[pl.ds(index, 1), :], (L, L)).T


def fold_rows(tile):
    return jnp.sum(tile.T, axis=0, keepdims=True)


def fold_sub(tile, op):
    return op(tile.reshape(L // 8, 8, L), axis=0)


def cols_of(c):
    return slice(c * L, (c + 1) * L)


def rows_of(r):
    if isinstance(r, int):
        return slice(r * L, (r + 1) * L)
    return pl.ds(pl.multiple_of(r * L, L), L)


def send(out_ref, lead, value):
    for n in range(out_ref.shape[0]):
        out_ref[(n,) + lead] = value


def copies(out_ref):
    for n in range(1, out_ref.shape[0]):
        out_ref[n] = out_ref[0]


def pack(left_ref, right_ref, a_ref, b_ref, scale):
    high, low = split(left_ref[...] * scale)
    for k, part in enumerate((high, high, low, low)):
        a_ref[:, cols_of(k)] = part
    high, low = split(right_ref[...])
    for k, part in enumerate((high, low, high, low)):
        b_ref[:, cols_of(k)] = part


def tiles(a_ref, b_ref, out_ref, rs, tile):
    cols = b_ref.shape[0]
    for c in range(0, cols, tile):
        out_ref[rs, c : c + tile] = lax.dot_general(
            a_ref[rs, :], b_ref[c : c + tile, :], (((1,), (1,)), ((), ())), preferred_element_type=F32
        )


def each_row(nr, body, unroll=ROW_UNROLL):
    if unroll >= nr:
        for r in range(nr):
            body(r)
        return

    def step(r, carry):
        body(r)
        return carry

    lax.fori_loop(0, nr, step, 0, unroll=min(unroll, nr))


def fetch(pairs, sem):
    moves = [pltpu.make_async_copy(src, dst, sem.at[n]) for n, (src, dst) in enumerate(pairs)]
    for move in moves:
        move.start()
    for move in moves:
        move.wait()


def planes(buf_ref):
    size = buf_ref.shape[1]
    return tuple(
        buf_ref.at[pl.ds(start, height), :]
        for start, height in ((0, size), (size, size), (2 * size, L), (2 * size + L, L))
    )


F1, S, IB, Q, H, Y, D = range(7)


def vec(buf_ref, name):
    size = buf_ref.shape[1]
    place = name % (size // L)
    return buf_ref.at[pl.ds(2 * size + 2 * L + (name // (size // L)) * (size // L), size // L), cols_of(place)]


def scores_kernel(scale, p_hbm, c_hbm, buf_ref, stat_ref, a_ref, b_ref, p_ref, c_ref, sem):
    fetch(((p_hbm, p_ref), (c_hbm, c_ref)), sem)
    pack(p_ref, c_ref, a_ref, b_ref, scale)
    z_ref = planes(buf_ref)[0]
    rows, nc = z_ref.shape[0], z_ref.shape[1] // L
    chunk = min(512, rows)
    for start in range(0, rows, chunk):
        tiles(a_ref, b_ref, z_ref, slice(start, start + chunk), min(1024, nc * L))
        for r in range(start // L, (start + chunk) // L):
            rs = slice(r * L, (r + 1) * L)
            top = z_ref[rs, cols_of(0)]
            for c in range(1, nc):
                top = jnp.maximum(top, z_ref[rs, cols_of(c)])
            peak = jnp.max(top.T, axis=0, keepdims=True)
            wide = jnp.broadcast_to(peak, (L, L)).T
            total = jnp.zeros((L, L), F32)
            for c in range(nc):
                total = total + jnp.exp(z_ref[rs, cols_of(c)] - wide)
            stat_ref[0, 0, r : r + 1, :] = peak
            stat_ref[0, 1, r : r + 1, :] = fold_rows(total)
    copies(stat_ref)


def merged(stat_ref):
    peak = stat_ref[0, 0]
    for n in range(1, stat_ref.shape[0]):
        peak = jnp.maximum(peak, stat_ref[n, 0])
    total = jnp.zeros_like(peak)
    for n in range(stat_ref.shape[0]):
        total = total + stat_ref[n, 1] * jnp.exp(stat_ref[n, 0] - peak)
    return peak + jnp.log(total)


def summed(ref, *lead):
    total = ref[(0,) + lead]
    for n in range(1, ref.shape[0]):
        total = total + ref[(n,) + lead]
    return total


def cols_kernel(
    old_ref, cot_hbm, c_hbm, rowstat_ref, buf_ref, stat_ref, peak_ref, total_ref, left_ref, right_ref,
    cot_ref, c_ref, sem
):
    fetch(((cot_hbm, cot_ref), (c_hbm, c_ref)), sem)
    b_ref = planes(old_ref)[0]
    w_ref = planes(buf_ref)[1]
    rows, cols = b_ref.shape
    nc = cols // L
    f1_ref = vec(buf_ref, F1)
    f1_ref[...] = -merged(rowstat_ref)
    peak_ref[...] = jnp.full_like(peak_ref, -jnp.inf)
    total_ref[...] = jnp.zeros_like(total_ref)
    pack(cot_ref, c_ref, left_ref, right_ref, 1.0)
    chunk = min(512, rows)
    for start in range(0, rows, chunk):
        tiles(left_ref, right_ref, w_ref, slice(start, start + chunk), min(1024, cols))
        for r in range(start // L, (start + chunk) // L):
            rs = slice(r * L, (r + 1) * L)
            shift = spread(f1_ref, r)
            for c in range(nc):
                cs = cols_of(c)
                shifted = b_ref[rs, cs] + shift
                old = peak_ref[:, cs]
                new = jnp.maximum(old, fold_sub(shifted, jnp.max))
                terms = jnp.exp(shifted.reshape(L // 8, 8, L) - new[None])
                total_ref[:, cs] = total_ref[:, cs] * jnp.exp(old - new) + jnp.sum(terms, axis=0)
                peak_ref[:, cs] = new
    for c in range(nc):
        cs = cols_of(c)
        peak = jnp.max(peak_ref[:, cs], axis=0, keepdims=True)
        total = jnp.sum(total_ref[:, cs] * jnp.exp(peak_ref[:, cs] - peak), axis=0, keepdims=True)
        stat_ref[0, 0, c : c + 1, :] = peak
        stat_ref[0, 1, c : c + 1, :] = total
    copies(stat_ref)


def plan_kernel(old_ref, colstat_ref, buf_ref, sum_ref, shift_ref, f1_ref):
    z_ref, out_ref = planes(old_ref)[0], planes(buf_ref)[0]
    nr, nc = z_ref.shape[0] // L, z_ref.shape[1] // L
    s_ref = vec(buf_ref, S)
    f1_ref[...] = vec(old_ref, F1)[...]
    lse = merged(colstat_ref)
    shift_ref[...] = -lse
    s_ref[...] = jnp.exp(lse)

    def body(r):
        shift = spread(f1_ref, r)
        waiting, totals = None, []
        for strip in range(0, L, 8):
            rs = pl.ds(pl.multiple_of(r * L + strip, 8), 8)
            row = shift[strip : strip + 8]
            values = [
                jnp.exp((z_ref[rs, cols_of(c)] + row) + shift_ref[c : c + 1, :]) for c in range(nc)
            ]
            totals.append(functools.reduce(jnp.add, values))
            put(out_ref, waiting)
            waiting = (rs, values)
        put(out_ref, waiting)
        sum_ref[0, pl.ds(r, 1), :] = fold_rows(jnp.concatenate(totals))

    each_row(nr, body, PLAN_UNROLL)
    copies(sum_ref)


def put(out_ref, waiting):
    if waiting is not None:
        for c, value in enumerate(waiting[1]):
            out_ref[waiting[0], cols_of(c)] = value


def edges_kernel(old_ref, rowsum_ref, buf_ref, stat_ref, one_ref, two_ref):
    b_ref, w_ref = planes(old_ref)[:2]
    nr, nc = b_ref.shape[0] // L, b_ref.shape[1] // L
    ib_ref = vec(buf_ref, IB)
    ib_ref[...] = 1.0 / summed(rowsum_ref)
    one_ref[...] = jnp.zeros_like(one_ref)
    two_ref[...] = jnp.zeros_like(two_ref)

    def body(r):
        rs = rows_of(r)
        inv = spread(ib_ref, r)
        for c in range(nc):
            cs = cols_of(c)
            value = b_ref[rs, cs] * inv
            one_ref[:, cs] += fold_sub(value, jnp.sum)
            two_ref[:, cs] += fold_sub(value * w_ref[rs, cs], jnp.sum)

    each_row(nr, body)
    for c in range(nc):
        cs = cols_of(c)
        stat_ref[0, 0, c : c + 1, :] = jnp.sum(one_ref[:, cs], axis=0, keepdims=True)
        stat_ref[0, 1, c : c + 1, :] = jnp.sum(two_ref[:, cs], axis=0, keepdims=True)
    copies(stat_ref)


def begin(pairs, sem):
    moves = [pltpu.make_async_copy(src, dst, sem.at[n]) for n, (src, dst) in enumerate(pairs)]
    for move in moves:
        move.start()
    return moves


def double(out_ref, r, value):
    high, low = split(value)
    chunk = out_ref.shape[2] // 2
    k, place = divmod(r * L, chunk)
    for start in (place, chunk + place):
        out_ref[k, :L, start : start + L] = high
        out_ref[k, L:, start : start + L] = low


def sweep(count, fill, use, slots):
    def both(filling, using):
        for one, other in itertools.zip_longest(filling, using):
            if one is not None:
                one()
            if other is not None:
                other()

    def body(j, carry):
        k = 2 * j
        both(fill(k + 1, slots[1]), use(k, slots[0]))
        both(fill(jnp.minimum(k + 2, count - 1), slots[0]), use(k + 1, slots[1]))
        return carry

    both(fill(0, slots[0]), [])
    lax.fori_loop(0, count // 2, body, 0)


def add_columns(left_ref, k, slot_ref, acc_ref, n):
    width = min(512, acc_ref.shape[1])
    ns = slice(n * width, (n + 1) * width)
    acc_ref[:, ns] += jnp.dot(left_ref[k], slot_ref[:, ns], preferred_element_type=F32)


def column_parts(acc_ref):
    return range(acc_ref.shape[1] // min(512, acc_ref.shape[1]))


def rowback_kernel(
    share, ratio, scale, old_ref, p_hbm, cot_hbm, colsum_ref, buf_ref, sum_ref,
    ct_ref, acc_ref, one_ref, two_ref, p_ref, cot_ref, sem
):
    moves = begin(((p_hbm, p_ref), (cot_hbm, cot_ref)), sem)
    b_ref, w_ref = planes(old_ref)[:2]
    pt_ref, direct_ref = planes(buf_ref)[2:]
    rows, cols = b_ref.shape
    nr, nc = rows // L, cols // L
    ib_ref, q_ref, h_ref = vec(old_ref, IB), vec(buf_ref, Q), vec(buf_ref, H)
    q = share / summed(colsum_ref, 0)
    q_ref[...] = q
    h_ref[...] = ratio * (q * summed(colsum_ref, 1))
    acc_ref[...] = jnp.zeros_like(acc_ref)

    def body(r):
        rs = rows_of(r)
        total = jnp.zeros((L, L), F32)
        for c in range(nc):
            cs = cols_of(c)
            total = total + (b_ref[rs, cs] * q_ref[c : c + 1, :]) * (w_ref[rs, cs] - h_ref[c : c + 1, :])
        sum_ref[0, pl.ds(r, 1), :] = fold_rows(total)

    each_row(nr, body)
    for move in moves:
        move.wait()
    for r in range(nr):
        rs = slice(r * L, (r + 1) * L)
        pt_ref[:, rs] = (p_ref[rs, :] * scale).T
        double(ct_ref, r, cot_ref[rs, :].T * ib_ref[r : r + 1, :])
    chunk = one_ref.shape[0] // 2

    def fill(k, slot_ref):
        def piece(sub):
            rs = rows_of(k * (chunk // L) + sub)
            for c in range(nc):
                high, low = split(b_ref[rs, cols_of(c)])
                slot_ref[sub * L : (sub + 1) * L, cols_of(c)] = high
                slot_ref[chunk + sub * L : chunk + (sub + 1) * L, cols_of(c)] = low

        return [functools.partial(piece, sub) for sub in range(chunk // L)]

    def use(k, slot_ref):
        return [functools.partial(add_columns, ct_ref, k, slot_ref, acc_ref, n) for n in column_parts(acc_ref)]

    sweep(rows // chunk, fill, use, (one_ref, two_ref))
    direct_ref[...] = acc_ref[:L, :] + acc_ref[L:, :]
    copies(sum_ref)


def colback_kernel(old_ref, rowsum_ref, buf_ref, sum_ref, acc_ref):
    b_ref = planes(old_ref)[0]
    nr, nc = b_ref.shape[0] // L, b_ref.shape[1] // L
    ib_ref, y_ref = vec(old_ref, IB), vec(buf_ref, Y)
    y_ref[...] = (summed(rowsum_ref) * ib_ref[...]) * ib_ref[...]
    acc_ref[...] = jnp.zeros_like(acc_ref)

    def body(r):
        rs = rows_of(r)
        y = spread(y_ref, r)
        for c in range(nc):
            cs = cols_of(c)
            acc_ref[:, cs] += fold_sub(b_ref[rs, cs] * y, jnp.sum)

    each_row(nr, body)
    for c in range(nc):
        sum_ref[0, c : c + 1, :] = -jnp.sum(acc_ref[:, cols_of(c)], axis=0, keepdims=True)
    copies(sum_ref)


def lastrow_kernel(old_ref, colsum_ref, buf_ref, sum_ref):
    b_ref = planes(old_ref)[0]
    nr, nc = b_ref.shape[0] // L, b_ref.shape[1] // L
    d_ref = vec(buf_ref, D)
    d_ref[...] = summed(colsum_ref)

    def body(r):
        rs = rows_of(r)
        total = jnp.zeros((L, L), F32)
        for c in range(nc):
            total = total + b_ref[rs, cols_of(c)] * d_ref[c : c + 1, :]
        sum_ref[0, pl.ds(r, 1), :] = -fold_rows(total)

    each_row(nr, body)
    copies(sum_ref)


def final_kernel(
    scale, old_ref, c_hbm, rowsum_ref, pg_ref, cg_ref,
    ib_ref, y_ref, f_ref, pt_ref, cc_ref, acc_ref, one_ref, two_ref, c_ref, sem
):
    moves = begin(((c_hbm, c_ref),), sem)
    b_ref, w_ref, p_ref, direct_ref = planes(old_ref)
    rows, cols = b_ref.shape
    nr, nc = rows // L, cols // L
    s_ref, q_ref, h_ref, d_ref = (vec(old_ref, name) for name in (S, Q, H, D))
    f_ref[...] = summed(rowsum_ref)
    ib_ref[...] = vec(old_ref, IB)[...]
    y_ref[...] = vec(old_ref, Y)[...]
    acc_ref[...] = jnp.zeros_like(acc_ref)
    for r in range(nr):
        double(pt_ref, r, p_ref[:, r * L : (r + 1) * L])
    for move in moves:
        move.wait()
    high, low = split(c_ref[...] * scale)
    cc_ref[:, :L] = high
    cc_ref[:, L:] = low
    chunk = one_ref.shape[0] // 2

    def fill(k, slot_ref):
        def piece(sub):
            r = k * (chunk // L) + sub
            rs = rows_of(r)
            inv, y, f = spread(ib_ref, r), spread(y_ref, r), spread(f_ref, r)
            for c in range(nc):
                row, cs = slice(c, c + 1), cols_of(c)
                plan = (q_ref[row, :] * inv) * (w_ref[rs, cs] - h_ref[row, :])
                factor = (y + d_ref[row, :]) + s_ref[row, :] * f
                high, low = split(b_ref[rs, cs] * (plan - factor))
                slot_ref[sub * L : (sub + 1) * L, cs] = high
                slot_ref[chunk + sub * L : chunk + (sub + 1) * L, cs] = low

        return [functools.partial(piece, sub) for sub in range(chunk // L)]

    def use(k, slot_ref):
        def points_part():
            both = jnp.dot(slot_ref[...], cc_ref[...], preferred_element_type=F32)
            both = both[:, :L] + both[:, L:]
            pg_ref[pl.ds(pl.multiple_of(k * chunk, chunk), chunk), :] = both[:chunk] + both[chunk:]

        parts = [functools.partial(add_columns, pt_ref, k, slot_ref, acc_ref, n) for n in column_parts(acc_ref)]
        return [points_part] + parts

    sweep(rows // chunk, fill, use, (one_ref, two_ref))
    for c in range(nc):
        cs = cols_of(c)
        plan = direct_ref[:, cs] * q_ref[c : c + 1, :]
        cg_ref[cs, :] = ((acc_ref[:L, cs] + acc_ref[L:, cs]) + plan).T


MIB = 1024 * 1024
LIMIT = 15 * MIB


def call(kernel, name, buf, fetched, args, outs, scratch=(), keep=True):
    whole = pl.BlockSpec(memory_space=pltpu.VMEM)
    outside = pl.BlockSpec(memory_space=pltpu.HBM)
    shapes = [jax.ShapeDtypeStruct(o, F32) for o in outs]
    specs = [outside] * len(fetched) + [whole] * len(args)
    args = [pltpu.with_memory_space_constraint(a, pltpu.HBM) for a in fetched] + args
    scratch = [pltpu.VMEM(s, t) for s, t in scratch]
    if fetched:
        scratch += [pltpu.VMEM(a.shape, F32) for a in fetched] + [pltpu.SemaphoreType.DMA((len(fetched),))]
    aliases = {}
    if isinstance(buf, tuple):
        shapes = [pltpu.VMEM(buf, F32)] + shapes
    else:
        args = [pltpu.with_memory_space_constraint(buf, pltpu.VMEM)] + args
        specs = [whole] + specs
        if keep:
            shapes = [pltpu.VMEM(buf.shape, F32)] + shapes
            aliases = {0: 0}
    return pl.pallas_call(
        kernel,
        name=name,
        out_shape=shapes,
        in_specs=specs,
        out_specs=[whole] * len(shapes),
        scratch_shapes=scratch,
        input_output_aliases=aliases,
        compiler_params=pltpu.CompilerParams(vmem_limit_bytes=LIMIT),
    )(*args)


def over(axis, value):
    return lax.all_to_all(value, axis, 0, 0, tiled=True)


def sizes():
    return lax.axis_size("pt"), lax.axis_size("ct")


def per_device(points, centroids, cotangent):
    rows, width = points.shape
    cols = centroids.shape[0]
    npt, nct = sizes()
    share = (rows * npt) / (cols * nct)
    ratio = (cols * nct) / (rows * npt)
    scale = 3.0 / math.sqrt(width)
    rvec, cvec = (rows // L, L), (cols // L, L)
    to_pt, to_ct = (npt,) + cvec, (nct,) + rvec
    tall = [((rows, 4 * L), BF16), ((cols, 4 * L), BF16)]
    strip = ((8, cols), F32)
    chunk = min(CHUNK, rows // 2)
    slot = ((2 * chunk, cols), BF16)
    doubles = ((rows // chunk, 2 * L, 2 * chunk), BF16)
    wide = ((2 * L, cols), F32)
    part = functools.partial

    extra = -(-7 // (cols // L)) * (cols // L)
    height = 2 * cols + 2 * L + -(-extra // 8) * 8
    buf, stat = call(
        part(scores_kernel, scale), "scores", (height, cols), [points, centroids], [],
        [(nct, 2) + rvec], tall,
    )
    stat = over("ct", stat)
    buf, stat = call(
        cols_kernel, "cols", buf, [cotangent, centroids], [stat],
        [(npt, 2) + cvec], [strip, strip] + tall,
    )
    stat = over("pt", stat)
    buf, sums = call(plan_kernel, "plan", buf, [], [stat], [to_ct], [(cvec, F32), (rvec, F32)])
    sums = over("ct", sums)
    buf, stat = call(edges_kernel, "edges", buf, [], [sums], [(npt, 2) + cvec], [strip, strip])
    stat = over("pt", stat)
    buf, sums = call(
        part(rowback_kernel, share, ratio, scale), "rowback", buf, [points, cotangent], [stat],
        [to_ct], [doubles, wide, slot, slot],
    )
    sums = over("ct", sums)
    buf, sums = call(colback_kernel, "colback", buf, [], [sums], [to_pt], [strip])
    sums = over("pt", sums)
    buf, sums = call(lastrow_kernel, "lastrow", buf, [], [sums], [to_ct])
    sums = over("ct", sums)
    pg, cg = call(
        part(final_kernel, scale), "final", buf, [centroids], [sums],
        [(rows, width), (cols, width)],
        [(rvec, F32), (rvec, F32), (rvec, F32), doubles, ((cols, 2 * L), BF16), wide, slot, slot],
        keep=False,
    )
    point_grad = gather_points(pg)
    cg = over("pt", cg.reshape(npt, cols // npt, width))
    cg = jnp.sum(cg, axis=0)
    cg = over("pt", jnp.broadcast_to(cg[None], (npt, cols // npt, width)))
    return (point_grad, cg.reshape(cols, width))


def gather_points(value):
    n = lax.axis_size("ct")
    me = lax.axis_index("ct")
    size = value.shape[0] // n
    total = lax.dynamic_slice_in_dim(value, me * size, size)
    for step in range(1, n):
        block = lax.dynamic_slice_in_dim(value, (me + step) % n * size, size)
        total = total + lax.ppermute(block, "ct", [(k, (k + step) % n) for k in range(n)])
    return total


def solution(mesh):
    return jax.shard_map(
        per_device,
        mesh=mesh,
        in_specs=(P("pt", None), P("ct", None), P("pt", None)),
        out_specs=(P(("pt", "ct"), None), P("ct", None)),
        check_vma=False,
    )
```

```python
import functools
import itertools
import math

import jax
import jax.numpy as jnp
from jax import lax
from jax.experimental import pallas as pl
from jax.experimental.pallas import tpu as pltpu
from jax.sharding import PartitionSpec as P

L = 128
F32 = jnp.float32
BF16 = jnp.bfloat16
ROW_UNROLL = 16
PLAN_UNROLL = 2
CHUNK = 256
GROUP = 2
PART = (512, 512)
WIDE = 512


def split(x):
    high = x.astype(BF16)
    return high, (x - high.astype(F32)).astype(BF16)


def spread(vec_ref, index):
    return jnp.broadcast_to(vec_ref[pl.ds(index, 1), :], (L, L)).T


def fold_rows(tile):
    return jnp.sum(tile.T, axis=0, keepdims=True)


def fold_sub(tile, op):
    return op(tile.reshape(L // 8, 8, L), axis=0)


def cols_of(c):
    return slice(c * L, (c + 1) * L)


def rows_of(r):
    if isinstance(r, int):
        return slice(r * L, (r + 1) * L)
    return pl.ds(pl.multiple_of(r * L, L), L)


def send(out_ref, lead, value):
    for n in range(out_ref.shape[0]):
        out_ref[(n,) + lead] = value


def copies(out_ref):
    for n in range(1, out_ref.shape[0]):
        out_ref[n] = out_ref[0]


LEFT, RIGHT = (0, 0, 1, 1), (0, 1, 0, 1)


def pack(value_ref, out_ref, order, scale):
    terms = split(value_ref[...] * scale)
    for k, term in enumerate(order):
        out_ref[:, cols_of(k)] = terms[term]


def parts_of(rows, cols):
    for r in range(0, rows, min(PART[0], rows)):
        for c in range(0, cols, min(PART[1], cols)):
            yield slice(r, r + min(PART[0], rows)), slice(c, c + min(PART[1], cols))


def tile(a_ref, b_ref, out_ref, rs, cs):
    out_ref[rs, cs] = lax.dot_general(
        a_ref[rs, :], b_ref[cs, :], (((1,), (1,)), ((), ())), preferred_element_type=F32
    )


def each_row(nr, body, unroll=ROW_UNROLL):
    if unroll >= nr:
        for r in range(nr):
            body(r)
        return

    def step(r, carry):
        body(r)
        return carry

    lax.fori_loop(0, nr, step, 0, unroll=min(unroll, nr))


def begin(pairs, sem):
    moves = [pltpu.make_async_copy(src, dst, sem.at[n]) for n, (src, dst) in enumerate(pairs)]
    for move in moves:
        move.start()
    return moves


def planes(buf_ref):
    size = buf_ref.shape[1]
    return tuple(
        buf_ref.at[pl.ds(start, height), :]
        for start, height in ((0, size), (size, size), (2 * size, L), (2 * size + L, L))
    )


F1, S, IB, Q, H, Y, D = range(7)


def vec(buf_ref, name):
    size = buf_ref.shape[1]
    place = name % (size // L)
    return buf_ref.at[pl.ds(2 * size + 2 * L + (name // (size // L)) * (size // L), size // L), cols_of(place)]


def scores_kernel(scale, p_hbm, c_hbm, buf_ref, stat_ref, a_ref, b_ref, p_ref, c_ref, sem):
    moves = begin(((p_hbm, p_ref), (c_hbm, c_ref)), sem)
    moves[0].wait()
    pack(p_ref, a_ref, LEFT, scale)
    moves[1].wait()
    pack(c_ref, b_ref, RIGHT, 1.0)
    z_ref = planes(buf_ref)[0]
    rows, cols = z_ref.shape
    nc = cols // L
    chunk = min(PART[0], rows)

    def sweep_row(r):
        rs = slice(r * L, (r + 1) * L)
        top = z_ref[rs, cols_of(0)]
        for c in range(1, nc):
            top = jnp.maximum(top, z_ref[rs, cols_of(c)])
        peak = jnp.max(top.T, axis=0, keepdims=True)
        wide = jnp.broadcast_to(peak, (L, L)).T
        total = jnp.zeros((L, L), F32)
        for c in range(nc):
            total = total + jnp.exp(z_ref[rs, cols_of(c)] - wide)
        stat_ref[0, r : r + 1, :] = peak + jnp.log(fold_rows(total))

    products = list(parts_of(rows, cols))
    each = len(products) * chunk // rows
    for rs, cs in products[:each]:
        tile(a_ref, b_ref, z_ref, rs, cs)
    for n in range(rows // chunk):
        coming = products[(n + 1) * each : (n + 2) * each]
        here = range(n * chunk // L, (n + 1) * chunk // L)
        done = 0
        for m, r in enumerate(here):
            until = len(coming) * (m + 1) // len(here)
            for rs, cs in coming[done:until]:
                tile(a_ref, b_ref, z_ref, rs, cs)
            done = until
            sweep_row(r)
    copies(stat_ref)


def merged(lse_ref):
    peak = lse_ref[0]
    for n in range(1, lse_ref.shape[0]):
        peak = jnp.maximum(peak, lse_ref[n])
    total = jnp.zeros_like(peak)
    for n in range(lse_ref.shape[0]):
        total = total + jnp.exp(lse_ref[n] - peak)
    return peak + jnp.log(total)


def summed(ref, *lead):
    total = ref[(0,) + lead]
    for n in range(1, ref.shape[0]):
        total = total + ref[(n,) + lead]
    return total


def cols_kernel(
    old_ref, cot_hbm, c_hbm, rowstat_ref, buf_ref, stat_ref, peak_ref, total_ref, left_ref, right_ref,
    cot_ref, c_ref, sem
):
    moves = begin(((cot_hbm, cot_ref), (c_hbm, c_ref)), sem)
    b_ref = planes(old_ref)[0]
    w_ref = planes(buf_ref)[1]
    rows, cols = b_ref.shape
    nc = cols // L
    f1_ref = vec(buf_ref, F1)
    f1_ref[...] = -merged(rowstat_ref)
    peak_ref[...] = jnp.full_like(peak_ref, -jnp.inf)
    total_ref[...] = jnp.zeros_like(total_ref)

    def sweep_row(r):
        rs = slice(r * L, (r + 1) * L)
        shift = spread(f1_ref, r)
        for c in range(nc):
            cs = cols_of(c)
            shifted = b_ref[rs, cs] + shift
            old = peak_ref[:, cs]
            new = jnp.maximum(old, fold_sub(shifted, jnp.max))
            terms = jnp.exp(shifted.reshape(L // 8, 8, L) - new[None])
            total_ref[:, cs] = total_ref[:, cs] * jnp.exp(old - new) + jnp.sum(terms, axis=0)
            peak_ref[:, cs] = new

    nr = rows // L
    early = nr // 4
    for r in range(early):
        sweep_row(r)
    for move in moves:
        move.wait()
    pack(cot_ref, left_ref, LEFT, 1.0)
    pack(c_ref, right_ref, RIGHT, 1.0)
    products = list(parts_of(rows, cols))
    done = 0
    for n, r in enumerate(range(early, nr)):
        until = len(products) * (n + 1) // (nr - early)
        for rs, cs in products[done:until]:
            tile(left_ref, right_ref, w_ref, rs, cs)
        done = until
        sweep_row(r)
    for c in range(nc):
        cs = cols_of(c)
        peak = jnp.max(peak_ref[:, cs], axis=0, keepdims=True)
        total = jnp.sum(total_ref[:, cs] * jnp.exp(peak_ref[:, cs] - peak), axis=0, keepdims=True)
        stat_ref[0, c : c + 1, :] = peak + jnp.log(total)
    copies(stat_ref)


def plan_kernel(old_ref, colstat_ref, buf_ref, sum_ref, shift_ref, f1_ref):
    z_ref, out_ref = planes(old_ref)[0], planes(buf_ref)[0]
    nr, nc = z_ref.shape[0] // L, z_ref.shape[1] // L
    s_ref = vec(buf_ref, S)
    f1_ref[...] = vec(old_ref, F1)[...]
    lse = merged(colstat_ref)
    shift_ref[...] = -lse
    s_ref[...] = jnp.exp(lse)

    def body(r):
        shift = spread(f1_ref, r)
        waiting, totals = None, []
        for strip in range(0, L, 8):
            rs = pl.ds(pl.multiple_of(r * L + strip, 8), 8)
            row = shift[strip : strip + 8]
            values = [
                jnp.exp((z_ref[rs, cols_of(c)] + row) + shift_ref[c : c + 1, :]) for c in range(nc)
            ]
            totals.append(functools.reduce(jnp.add, values))
            put(out_ref, waiting)
            waiting = (rs, values)
        put(out_ref, waiting)
        sum_ref[0, pl.ds(r, 1), :] = fold_rows(jnp.concatenate(totals))

    each_row(nr, body, PLAN_UNROLL)
    copies(sum_ref)


def put(out_ref, waiting):
    if waiting is not None:
        for c, value in enumerate(waiting[1]):
            out_ref[waiting[0], cols_of(c)] = value


def edges_kernel(old_ref, rowsum_ref, buf_ref, stat_ref, one_ref, two_ref):
    b_ref, w_ref = planes(old_ref)[:2]
    nr, nc = b_ref.shape[0] // L, b_ref.shape[1] // L
    ib_ref = vec(buf_ref, IB)
    ib_ref[...] = 1.0 / summed(rowsum_ref)
    one_ref[...] = jnp.zeros_like(one_ref)
    two_ref[...] = jnp.zeros_like(two_ref)

    def body(r):
        rs = rows_of(r)
        inv = spread(ib_ref, r)
        for c in range(nc):
            cs = cols_of(c)
            value = b_ref[rs, cs] * inv
            one_ref[:, cs] += fold_sub(value, jnp.sum)
            two_ref[:, cs] += fold_sub(value * w_ref[rs, cs], jnp.sum)

    each_row(nr, body)
    for c in range(nc):
        cs = cols_of(c)
        stat_ref[0, 0, c : c + 1, :] = jnp.sum(one_ref[:, cs], axis=0, keepdims=True)
        stat_ref[0, 1, c : c + 1, :] = jnp.sum(two_ref[:, cs], axis=0, keepdims=True)
    copies(stat_ref)


def double(out_ref, r, value):
    high, low = split(value)
    chunk = out_ref.shape[2] // 2
    k, place = divmod(r * L, chunk)
    for start in (place, chunk + place):
        out_ref[k, :L, start : start + L] = high
        out_ref[k, L:, start : start + L] = low


def sweep(count, fill, use, slots):
    def both(filling, using):
        for one, other in itertools.zip_longest(filling, using):
            if one is not None:
                one()
            if other is not None:
                other()

    def body(j, carry):
        k = 2 * j
        both(fill(k + 1, slots[1]), use(k, slots[0]))
        both(fill(jnp.minimum(k + 2, count - 1), slots[0]), use(k + 1, slots[1]))
        return carry

    both(fill(0, slots[0]), [])
    lax.fori_loop(0, count // 2, body, 0)


def pieces(piece, count, nc):
    groups = [range(c, min(c + GROUP, nc)) for c in range(0, nc, GROUP)]
    return [functools.partial(piece, sub, group) for sub in range(count) for group in groups]


def add_columns(left_ref, k, slot_ref, acc_ref, n):
    width = min(WIDE, acc_ref.shape[1])
    ns = slice(n * width, (n + 1) * width)
    acc_ref[:, ns] += jnp.dot(left_ref[k], slot_ref[:, ns], preferred_element_type=F32)


def column_parts(acc_ref):
    return range(acc_ref.shape[1] // min(WIDE, acc_ref.shape[1]))


def rowback_kernel(
    share, ratio, scale, old_ref, p_hbm, cot_hbm, colsum_ref, buf_ref, sum_ref,
    ct_ref, acc_ref, one_ref, two_ref, p_ref, cot_ref, sem
):
    moves = begin(((p_hbm, p_ref), (cot_hbm, cot_ref)), sem)
    b_ref, w_ref = planes(old_ref)[:2]
    pt_ref, direct_ref = planes(buf_ref)[2:]
    rows, cols = b_ref.shape
    nr, nc = rows // L, cols // L
    ib_ref, q_ref, h_ref = vec(old_ref, IB), vec(buf_ref, Q), vec(buf_ref, H)
    q = share / summed(colsum_ref, 0)
    q_ref[...] = q
    h_ref[...] = ratio * (q * summed(colsum_ref, 1))
    acc_ref[...] = jnp.zeros_like(acc_ref)

    def body(r):
        rs = rows_of(r)
        total = jnp.zeros((L, L), F32)
        for c in range(nc):
            cs = cols_of(c)
            total = total + (b_ref[rs, cs] * q_ref[c : c + 1, :]) * (w_ref[rs, cs] - h_ref[c : c + 1, :])
        sum_ref[0, pl.ds(r, 1), :] = fold_rows(total)

    each_row(nr, body)
    for move in moves:
        move.wait()
    for r in range(nr):
        rs = slice(r * L, (r + 1) * L)
        pt_ref[:, rs] = (p_ref[rs, :] * scale).T
        double(ct_ref, r, cot_ref[rs, :].T * ib_ref[r : r + 1, :])
    chunk = one_ref.shape[0] // 2

    def fill(k, slot_ref):
        def piece(sub, group):
            rs = rows_of(k * (chunk // L) + sub)
            for c in group:
                high, low = split(b_ref[rs, cols_of(c)])
                slot_ref[sub * L : (sub + 1) * L, cols_of(c)] = high
                slot_ref[chunk + sub * L : chunk + (sub + 1) * L, cols_of(c)] = low

        return pieces(piece, chunk // L, nc)

    def use(k, slot_ref):
        return [functools.partial(add_columns, ct_ref, k, slot_ref, acc_ref, n) for n in column_parts(acc_ref)]

    sweep(rows // chunk, fill, use, (one_ref, two_ref))
    direct_ref[...] = acc_ref[:L, :] + acc_ref[L:, :]
    copies(sum_ref)


def colback_kernel(old_ref, rowsum_ref, buf_ref, sum_ref, acc_ref):
    b_ref = planes(old_ref)[0]
    nr, nc = b_ref.shape[0] // L, b_ref.shape[1] // L
    ib_ref, y_ref = vec(old_ref, IB), vec(buf_ref, Y)
    y_ref[...] = (summed(rowsum_ref) * ib_ref[...]) * ib_ref[...]
    acc_ref[...] = jnp.zeros_like(acc_ref)

    def body(r):
        rs = rows_of(r)
        y = spread(y_ref, r)
        for c in range(nc):
            cs = cols_of(c)
            acc_ref[:, cs] += fold_sub(b_ref[rs, cs] * y, jnp.sum)

    each_row(nr, body)
    for c in range(nc):
        sum_ref[0, c : c + 1, :] = -jnp.sum(acc_ref[:, cols_of(c)], axis=0, keepdims=True)
    copies(sum_ref)


def lastrow_kernel(old_ref, colsum_ref, buf_ref, sum_ref):
    b_ref = planes(old_ref)[0]
    nr, nc = b_ref.shape[0] // L, b_ref.shape[1] // L
    d_ref = vec(buf_ref, D)
    d_ref[...] = summed(colsum_ref)

    def body(r):
        rs = rows_of(r)
        total = jnp.zeros((L, L), F32)
        for c in range(nc):
            total = total + b_ref[rs, cols_of(c)] * d_ref[c : c + 1, :]
        sum_ref[0, pl.ds(r, 1), :] = -fold_rows(total)

    each_row(nr, body)
    copies(sum_ref)


def final_kernel(
    scale, old_ref, c_hbm, rowsum_ref, pg_ref, cg_ref,
    ib_ref, y_ref, f_ref, pt_ref, cc_ref, acc_ref, one_ref, two_ref, c_ref, sem
):
    moves = begin(((c_hbm, c_ref),), sem)
    b_ref, w_ref, p_ref, direct_ref = planes(old_ref)
    rows, cols = b_ref.shape
    nr, nc = rows // L, cols // L
    s_ref, q_ref, h_ref, d_ref = (vec(old_ref, name) for name in (S, Q, H, D))
    f_ref[...] = summed(rowsum_ref)
    ib_ref[...] = vec(old_ref, IB)[...]
    y_ref[...] = vec(old_ref, Y)[...]
    acc_ref[...] = jnp.zeros_like(acc_ref)
    for r in range(nr):
        double(pt_ref, r, p_ref[:, r * L : (r + 1) * L])
    for move in moves:
        move.wait()
    high, low = split(c_ref[...] * scale)
    cc_ref[:, :L] = high
    cc_ref[:, L:] = low
    chunk = one_ref.shape[0] // 2

    def fill(k, slot_ref):
        def piece(sub, group):
            r = k * (chunk // L) + sub
            rs = rows_of(r)
            inv, y, f = spread(ib_ref, r), spread(y_ref, r), spread(f_ref, r)
            for c in group:
                row, cs = slice(c, c + 1), cols_of(c)
                plan = (q_ref[row, :] * inv) * (w_ref[rs, cs] - h_ref[row, :])
                factor = (y + d_ref[row, :]) + s_ref[row, :] * f
                high, low = split(b_ref[rs, cs] * (plan - factor))
                slot_ref[sub * L : (sub + 1) * L, cs] = high
                slot_ref[chunk + sub * L : chunk + (sub + 1) * L, cs] = low

        return pieces(piece, chunk // L, nc)

    def use(k, slot_ref):
        def points_part():
            both = jnp.dot(slot_ref[...], cc_ref[...], preferred_element_type=F32)
            both = both[:, :L] + both[:, L:]
            pg_ref[pl.ds(pl.multiple_of(k * chunk, chunk), chunk), :] = both[:chunk] + both[chunk:]

        parts = [functools.partial(add_columns, pt_ref, k, slot_ref, acc_ref, n) for n in column_parts(acc_ref)]
        return [points_part] + parts

    sweep(rows // chunk, fill, use, (one_ref, two_ref))
    for c in range(nc):
        cs = cols_of(c)
        plan = direct_ref[:, cs] * q_ref[c : c + 1, :]
        cg_ref[cs, :] = ((acc_ref[:L, cs] + acc_ref[L:, cs]) + plan).T


MIB = 1024 * 1024
LIMIT = 15 * MIB


def call(kernel, name, buf, fetched, args, outs, scratch=(), keep=True):
    whole = pl.BlockSpec(memory_space=pltpu.VMEM)
    outside = pl.BlockSpec(memory_space=pltpu.HBM)
    shapes = [jax.ShapeDtypeStruct(o, F32) for o in outs]
    specs = [outside] * len(fetched) + [whole] * len(args)
    args = [pltpu.with_memory_space_constraint(a, pltpu.HBM) for a in fetched] + args
    scratch = [pltpu.VMEM(s, t) for s, t in scratch]
    if fetched:
        scratch += [pltpu.VMEM(a.shape, F32) for a in fetched] + [pltpu.SemaphoreType.DMA((len(fetched),))]
    aliases = {}
    if isinstance(buf, tuple):
        shapes = [pltpu.VMEM(buf, F32)] + shapes
    else:
        args = [pltpu.with_memory_space_constraint(buf, pltpu.VMEM)] + args
        specs = [whole] + specs
        if keep:
            shapes = [pltpu.VMEM(buf.shape, F32)] + shapes
            aliases = {0: 0}
    return pl.pallas_call(
        kernel,
        name=name,
        out_shape=shapes,
        in_specs=specs,
        out_specs=[whole] * len(shapes),
        scratch_shapes=scratch,
        input_output_aliases=aliases,
        compiler_params=pltpu.CompilerParams(vmem_limit_bytes=LIMIT),
    )(*args)


def over(axis, value):
    return lax.all_to_all(value, axis, 0, 0, tiled=True)


def sizes():
    return lax.axis_size("pt"), lax.axis_size("ct")


def per_device(points, centroids, cotangent):
    rows, width = points.shape
    cols = centroids.shape[0]
    npt, nct = sizes()
    share = (rows * npt) / (cols * nct)
    ratio = (cols * nct) / (rows * npt)
    scale = 3.0 / math.sqrt(width)
    rvec, cvec = (rows // L, L), (cols // L, L)
    to_pt, to_ct = (npt,) + cvec, (nct,) + rvec
    tall = [((rows, 4 * L), BF16), ((cols, 4 * L), BF16)]
    strip = ((8, cols), F32)
    chunk = min(CHUNK, rows // 2)
    slot = ((2 * chunk, cols), BF16)
    doubles = ((rows // chunk, 2 * L, 2 * chunk), BF16)
    wide = ((2 * L, cols), F32)
    part = functools.partial

    extra = -(-7 // (cols // L)) * (cols // L)
    height = 2 * cols + 2 * L + -(-extra // 8) * 8
    buf, stat = call(
        part(scores_kernel, scale), "scores", (height, cols), [points, centroids], [],
        [to_ct], tall,
    )
    stat = over("ct", stat)
    buf, stat = call(
        cols_kernel, "cols", buf, [cotangent, centroids], [stat],
        [to_pt], [strip, strip] + tall,
    )
    stat = over("pt", stat)
    buf, sums = call(plan_kernel, "plan", buf, [], [stat], [to_ct], [(cvec, F32), (rvec, F32)])
    sums = over("ct", sums)
    buf, stat = call(edges_kernel, "edges", buf, [], [sums], [(npt, 2) + cvec], [strip, strip])
    stat = over("pt", stat)
    buf, sums = call(
        part(rowback_kernel, share, ratio, scale), "rowback", buf, [points, cotangent], [stat],
        [to_ct], [doubles, wide, slot, slot],
    )
    sums = over("ct", sums)
    buf, sums = call(colback_kernel, "colback", buf, [], [sums], [to_pt], [strip])
    sums = over("pt", sums)
    buf, sums = call(lastrow_kernel, "lastrow", buf, [], [sums], [to_ct])
    sums = over("ct", sums)
    pg, cg = call(
        part(final_kernel, scale), "final", buf, [centroids], [sums],
        [(rows, width), (cols, width)],
        [(rvec, F32), (rvec, F32), (rvec, F32), doubles, ((cols, 2 * L), BF16), wide, slot, slot],
        keep=False,
    )
    point_grad = gather_points(pg)
    cg = over("pt", cg.reshape(npt, cols // npt, width))
    cg = jnp.sum(cg, axis=0)
    cg = over("pt", jnp.broadcast_to(cg[None], (npt, cols // npt, width)))
    return (point_grad, cg.reshape(cols, width))


def gather_points(value):
    n = lax.axis_size("ct")
    me = lax.axis_index("ct")
    size = value.shape[0] // n
    total = lax.dynamic_slice_in_dim(value, me * size, size)
    for step in range(1, n):
        block = lax.dynamic_slice_in_dim(value, (me + step) % n * size, size)
        total = total + lax.ppermute(block, "ct", [(k, (k + step) % n) for k in range(n)])
    return total


def solution(mesh):
    return jax.shard_map(
        per_device,
        mesh=mesh,
        in_specs=(P("pt", None), P("ct", None), P("pt", None)),
        out_specs=(P(("pt", "ct"), None), P("ct", None)),
        check_vma=False,
    )
```

```python
import functools
import itertools
import math

import jax
import jax.numpy as jnp
from jax import lax
from jax.experimental import pallas as pl
from jax.experimental.pallas import tpu as pltpu
from jax.sharding import PartitionSpec as P

L = 128
F32 = jnp.float32
BF16 = jnp.bfloat16
ROW_UNROLL = 16
PLAN_UNROLL = 8
CHUNK = 256
GROUP = 2
PART = (512, 512)
WIDE = 512


def split(x):
    high = x.astype(BF16)
    return high, (x - high.astype(F32)).astype(BF16)


def spread(vec_ref, index):
    return jnp.broadcast_to(vec_ref[pl.ds(index, 1), :], (L, L)).T


def fold_rows(tile):
    return jnp.sum(tile.T, axis=0, keepdims=True)


def fold_sub(tile, op):
    return op(tile.reshape(L // 8, 8, L), axis=0)


def cols_of(c):
    return slice(c * L, (c + 1) * L)


def rows_of(r):
    if isinstance(r, int):
        return slice(r * L, (r + 1) * L)
    return pl.ds(pl.multiple_of(r * L, L), L)


def send(out_ref, lead, value):
    for n in range(out_ref.shape[0]):
        out_ref[(n,) + lead] = value


def copies(out_ref):
    for n in range(1, out_ref.shape[0]):
        out_ref[n] = out_ref[0]


LEFT, RIGHT = (0, 0, 1, 1), (0, 1, 0, 1)


def pack(value_ref, out_ref, order, scale):
    terms = split(value_ref[...] * scale)
    for k, term in enumerate(order):
        out_ref[:, cols_of(k)] = terms[term]


def parts_of(rows, cols):
    for r in range(0, rows, min(PART[0], rows)):
        for c in range(0, cols, min(PART[1], cols)):
            yield slice(r, r + min(PART[0], rows)), slice(c, c + min(PART[1], cols))


def tile(a_ref, b_ref, out_ref, rs, cs):
    out_ref[rs, cs] = lax.dot_general(
        a_ref[rs, :], b_ref[cs, :], (((1,), (1,)), ((), ())), preferred_element_type=F32
    )


def each_row(nr, body, unroll=ROW_UNROLL):
    if unroll >= nr:
        for r in range(nr):
            body(r)
        return

    def step(r, carry):
        body(r)
        return carry

    lax.fori_loop(0, nr, step, 0, unroll=min(unroll, nr))


def begin(pairs, sem):
    moves = [pltpu.make_async_copy(src, dst, sem.at[n]) for n, (src, dst) in enumerate(pairs)]
    for move in moves:
        move.start()
    return moves


def planes(buf_ref):
    size = buf_ref.shape[1]
    return tuple(
        buf_ref.at[pl.ds(start, height), :]
        for start, height in ((0, size), (size, size), (2 * size, L), (2 * size + L, L))
    )


F1, S, IB, Q, H, Y, D = range(7)


def vec(buf_ref, name):
    size = buf_ref.shape[1]
    place = name % (size // L)
    return buf_ref.at[pl.ds(2 * size + 2 * L + (name // (size // L)) * (size // L), size // L), cols_of(place)]


def scores_kernel(scale, p_hbm, c_hbm, buf_ref, stat_ref, a_ref, b_ref, p_ref, c_ref, sem):
    moves = begin(((p_hbm, p_ref), (c_hbm, c_ref)), sem)
    moves[0].wait()
    pack(p_ref, a_ref, LEFT, scale * math.log2(math.e))
    moves[1].wait()
    pack(c_ref, b_ref, RIGHT, 1.0)
    z_ref = planes(buf_ref)[0]
    rows, cols = z_ref.shape
    nc = cols // L
    chunk = min(PART[0], rows)

    def sweep_row(r):
        rs = slice(r * L, (r + 1) * L)
        top = z_ref[rs, cols_of(0)]
        for c in range(1, nc):
            top = jnp.maximum(top, z_ref[rs, cols_of(c)])
        peak = jnp.max(top.T, axis=0, keepdims=True)
        wide = jnp.broadcast_to(peak, (L, L)).T
        total = jnp.zeros((L, L), F32)
        for c in range(nc):
            total = total + jnp.exp2(z_ref[rs, cols_of(c)] - wide)
        stat_ref[0, r : r + 1, :] = peak + jnp.log2(fold_rows(total))

    products = list(parts_of(rows, cols))
    each = len(products) * chunk // rows
    for rs, cs in products[:each]:
        tile(a_ref, b_ref, z_ref, rs, cs)
    for n in range(rows // chunk):
        coming = products[(n + 1) * each : (n + 2) * each]
        here = range(n * chunk // L, (n + 1) * chunk // L)
        done = 0
        for m, r in enumerate(here):
            until = len(coming) * (m + 1) // len(here)
            for rs, cs in coming[done:until]:
                tile(a_ref, b_ref, z_ref, rs, cs)
            done = until
            sweep_row(r)
    copies(stat_ref)


def merged(lse_ref):
    peak = lse_ref[0]
    for n in range(1, lse_ref.shape[0]):
        peak = jnp.maximum(peak, lse_ref[n])
    total = jnp.zeros_like(peak)
    for n in range(lse_ref.shape[0]):
        total = total + jnp.exp2(lse_ref[n] - peak)
    return peak + jnp.log2(total)


def summed(ref, *lead):
    total = ref[(0,) + lead]
    for n in range(1, ref.shape[0]):
        total = total + ref[(n,) + lead]
    return total


def cols_kernel(
    old_ref, cot_hbm, c_hbm, rowstat_ref, buf_ref, stat_ref, peak_ref, total_ref, left_ref, right_ref,
    cot_ref, c_ref, sem
):
    moves = begin(((cot_hbm, cot_ref), (c_hbm, c_ref)), sem)
    b_ref = planes(old_ref)[0]
    w_ref = planes(buf_ref)[1]
    rows, cols = b_ref.shape
    nc = cols // L
    f1_ref = vec(buf_ref, F1)
    f1_ref[...] = -merged(rowstat_ref)
    peak_ref[...] = jnp.full_like(peak_ref, -jnp.inf)
    total_ref[...] = jnp.zeros_like(total_ref)

    def sweep_row(r):
        rs = slice(r * L, (r + 1) * L)
        shift = spread(f1_ref, r)
        for c in range(nc):
            cs = cols_of(c)
            shifted = b_ref[rs, cs] + shift
            old = peak_ref[:, cs]
            new = jnp.maximum(old, fold_sub(shifted, jnp.max))
            terms = jnp.exp2(shifted.reshape(L // 8, 8, L) - new[None])
            total_ref[:, cs] = total_ref[:, cs] * jnp.exp2(old - new) + jnp.sum(terms, axis=0)
            peak_ref[:, cs] = new

    nr = rows // L
    early = nr // 4
    for r in range(early):
        sweep_row(r)
    for move in moves:
        move.wait()
    pack(cot_ref, left_ref, LEFT, 1.0)
    pack(c_ref, right_ref, RIGHT, 1.0)
    products = list(parts_of(rows, cols))
    done = 0
    for n, r in enumerate(range(early, nr)):
        until = len(products) * (n + 1) // (nr - early)
        for rs, cs in products[done:until]:
            tile(left_ref, right_ref, w_ref, rs, cs)
        done = until
        sweep_row(r)
    for c in range(nc):
        cs = cols_of(c)
        peak = jnp.max(peak_ref[:, cs], axis=0, keepdims=True)
        total = jnp.sum(total_ref[:, cs] * jnp.exp2(peak_ref[:, cs] - peak), axis=0, keepdims=True)
        stat_ref[0, c : c + 1, :] = peak + jnp.log2(total)
    copies(stat_ref)


def plan_kernel(old_ref, colstat_ref, buf_ref, sum_ref, shift_ref, f1_ref):
    z_ref, out_ref = planes(old_ref)[0], planes(buf_ref)[0]
    nr, nc = z_ref.shape[0] // L, z_ref.shape[1] // L
    s_ref = vec(buf_ref, S)
    f1_ref[...] = vec(old_ref, F1)[...]
    lse = merged(colstat_ref)
    shift_ref[...] = -lse
    s_ref[...] = jnp.exp2(lse)

    def body(r):
        shift = spread(f1_ref, r)
        waiting, totals = None, []
        for strip in range(0, L, 8):
            rs = pl.ds(pl.multiple_of(r * L + strip, 8), 8)
            row = shift[strip : strip + 8]
            values = [
                jnp.exp2((z_ref[rs, cols_of(c)] + row) + shift_ref[c : c + 1, :]) for c in range(nc)
            ]
            totals.append(functools.reduce(jnp.add, values))
            put(out_ref, waiting)
            waiting = (rs, values)
        put(out_ref, waiting)
        sum_ref[0, pl.ds(r, 1), :] = fold_rows(jnp.concatenate(totals))

    each_row(nr, body, PLAN_UNROLL)
    copies(sum_ref)


def put(out_ref, waiting):
    if waiting is not None:
        for c, value in enumerate(waiting[1]):
            out_ref[waiting[0], cols_of(c)] = value


def edges_kernel(old_ref, rowsum_ref, buf_ref, stat_ref, one_ref, two_ref):
    b_ref, w_ref = planes(old_ref)[:2]
    nr, nc = b_ref.shape[0] // L, b_ref.shape[1] // L
    ib_ref = vec(buf_ref, IB)
    ib_ref[...] = 1.0 / summed(rowsum_ref)
    one_ref[...] = jnp.zeros_like(one_ref)
    two_ref[...] = jnp.zeros_like(two_ref)

    def body(r):
        rs = rows_of(r)
        inv = spread(ib_ref, r)
        for c in range(nc):
            cs = cols_of(c)
            value = b_ref[rs, cs] * inv
            one_ref[:, cs] += fold_sub(value, jnp.sum)
            two_ref[:, cs] += fold_sub(value * w_ref[rs, cs], jnp.sum)

    each_row(nr, body)
    for c in range(nc):
        cs = cols_of(c)
        stat_ref[0, 0, c : c + 1, :] = jnp.sum(one_ref[:, cs], axis=0, keepdims=True)
        stat_ref[0, 1, c : c + 1, :] = jnp.sum(two_ref[:, cs], axis=0, keepdims=True)
    copies(stat_ref)


def double(out_ref, r, value):
    high, low = split(value)
    chunk = out_ref.shape[2] // 2
    k, place = divmod(r * L, chunk)
    out_ref[k, :L, place : place + L] = high
    out_ref[k, L:, place : place + L] = low
    out_ref[k, :L, chunk + place : chunk + place + L] = high


def sweep(count, fill, use, slots):
    def both(filling, using):
        for one, other in itertools.zip_longest(filling, using):
            if one is not None:
                one()
            if other is not None:
                other()

    def body(j, carry):
        k = 2 * j
        both(fill(k + 1, slots[1]), use(k, slots[0]))
        both(fill(k + 2, slots[0]), use(k + 1, slots[1]))
        return carry

    both(fill(0, slots[0]), [])
    lax.fori_loop(0, count // 2 - 1, body, 0)
    both(fill(count - 1, slots[1]), use(count - 2, slots[0]))
    for other in use(count - 1, slots[1]):
        other()


def pieces(piece, count, nc):
    groups = [range(c, min(c + GROUP, nc)) for c in range(0, nc, GROUP)]
    return [functools.partial(piece, sub, group) for sub in range(count) for group in groups]


def add_columns(left_ref, k, slot_ref, acc_ref, n):
    width = min(WIDE, acc_ref.shape[1])
    ns = slice(n * width, (n + 1) * width)
    chunk = slot_ref.shape[0] // 2
    acc_ref[:, ns] += jnp.dot(left_ref[k, :, :chunk], slot_ref[:chunk, ns], preferred_element_type=F32)
    acc_ref[:L, ns] += jnp.dot(left_ref[k, :L, chunk:], slot_ref[chunk:, ns], preferred_element_type=F32)


def column_parts(acc_ref):
    return range(acc_ref.shape[1] // min(WIDE, acc_ref.shape[1]))


def rowback_kernel(
    share, ratio, scale, old_ref, p_hbm, cot_hbm, colsum_ref, buf_ref, sum_ref,
    ct_ref, acc_ref, one_ref, two_ref, p_ref, cot_ref, sem
):
    moves = begin(((p_hbm, p_ref), (cot_hbm, cot_ref)), sem)
    b_ref, w_ref = planes(old_ref)[:2]
    pt_ref, direct_ref = planes(buf_ref)[2:]
    rows, cols = b_ref.shape
    nr, nc = rows // L, cols // L
    ib_ref, q_ref, h_ref = vec(old_ref, IB), vec(buf_ref, Q), vec(buf_ref, H)
    q = share / summed(colsum_ref, 0)
    q_ref[...] = q
    h_ref[...] = ratio * (q * summed(colsum_ref, 1))
    acc_ref[...] = jnp.zeros_like(acc_ref)

    def body(r):
        rs = rows_of(r)
        total = jnp.zeros((L, L), F32)
        for c in range(nc):
            cs = cols_of(c)
            total = total + (b_ref[rs, cs] * q_ref[c : c + 1, :]) * (w_ref[rs, cs] - h_ref[c : c + 1, :])
        sum_ref[0, pl.ds(r, 1), :] = fold_rows(total)

    each_row(nr, body)
    for move in moves:
        move.wait()
    for r in range(nr):
        rs = slice(r * L, (r + 1) * L)
        pt_ref[:, rs] = (p_ref[rs, :] * scale).T
        double(ct_ref, r, cot_ref[rs, :].T * ib_ref[r : r + 1, :])
    chunk = one_ref.shape[0] // 2

    def fill(k, slot_ref):
        def piece(sub, group):
            rs = rows_of(k * (chunk // L) + sub)
            for c in group:
                high, low = split(b_ref[rs, cols_of(c)])
                slot_ref[sub * L : (sub + 1) * L, cols_of(c)] = high
                slot_ref[chunk + sub * L : chunk + (sub + 1) * L, cols_of(c)] = low

        return pieces(piece, chunk // L, nc)

    def use(k, slot_ref):
        return [functools.partial(add_columns, ct_ref, k, slot_ref, acc_ref, n) for n in column_parts(acc_ref)]

    sweep(rows // chunk, fill, use, (one_ref, two_ref))
    direct_ref[...] = acc_ref[:L, :] + acc_ref[L:, :]
    copies(sum_ref)


def colback_kernel(old_ref, rowsum_ref, buf_ref, sum_ref, acc_ref):
    b_ref = planes(old_ref)[0]
    nr, nc = b_ref.shape[0] // L, b_ref.shape[1] // L
    ib_ref, y_ref = vec(old_ref, IB), vec(buf_ref, Y)
    y_ref[...] = (summed(rowsum_ref) * ib_ref[...]) * ib_ref[...]
    acc_ref[...] = jnp.zeros_like(acc_ref)

    def body(r):
        rs = rows_of(r)
        y = spread(y_ref, r)
        for c in range(nc):
            cs = cols_of(c)
            acc_ref[:, cs] += fold_sub(b_ref[rs, cs] * y, jnp.sum)

    each_row(nr, body)
    for c in range(nc):
        sum_ref[0, c : c + 1, :] = -jnp.sum(acc_ref[:, cols_of(c)], axis=0, keepdims=True)
    copies(sum_ref)


def lastrow_kernel(old_ref, colsum_ref, buf_ref, sum_ref):
    b_ref = planes(old_ref)[0]
    nr, nc = b_ref.shape[0] // L, b_ref.shape[1] // L
    d_ref = vec(buf_ref, D)
    d_ref[...] = summed(colsum_ref)

    def body(r):
        rs = rows_of(r)
        total = jnp.zeros((L, L), F32)
        for c in range(nc):
            total = total + b_ref[rs, cols_of(c)] * d_ref[c : c + 1, :]
        sum_ref[0, pl.ds(r, 1), :] = -fold_rows(total)

    each_row(nr, body)
    copies(sum_ref)


def final_kernel(
    scale, old_ref, c_hbm, rowsum_ref, pg_ref, cg_ref,
    ib_ref, y_ref, f_ref, pt_ref, cc_ref, acc_ref, one_ref, two_ref, c_ref, sem
):
    moves = begin(((c_hbm, c_ref),), sem)
    b_ref, w_ref, p_ref, direct_ref = planes(old_ref)
    rows, cols = b_ref.shape
    nr, nc = rows // L, cols // L
    s_ref, q_ref, h_ref, d_ref = (vec(old_ref, name) for name in (S, Q, H, D))
    f_ref[...] = summed(rowsum_ref)
    ib_ref[...] = vec(old_ref, IB)[...]
    y_ref[...] = vec(old_ref, Y)[...]
    acc_ref[...] = jnp.zeros_like(acc_ref)
    for r in range(nr):
        double(pt_ref, r, p_ref[:, r * L : (r + 1) * L])
    for move in moves:
        move.wait()
    high, low = split(c_ref[...] * scale)
    cc_ref[:, :L] = high
    cc_ref[:, L:] = low
    chunk = one_ref.shape[0] // 2

    def fill(k, slot_ref):
        def piece(sub, group):
            r = k * (chunk // L) + sub
            rs = rows_of(r)
            inv, y, f = spread(ib_ref, r), spread(y_ref, r), spread(f_ref, r)
            for c in group:
                row, cs = slice(c, c + 1), cols_of(c)
                plan = (q_ref[row, :] * inv) * (w_ref[rs, cs] - h_ref[row, :])
                factor = (y + d_ref[row, :]) + s_ref[row, :] * f
                high, low = split(b_ref[rs, cs] * (plan - factor))
                slot_ref[sub * L : (sub + 1) * L, cs] = high
                slot_ref[chunk + sub * L : chunk + (sub + 1) * L, cs] = low

        return pieces(piece, chunk // L, nc)

    def use(k, slot_ref):
        def points_part():
            both = jnp.dot(slot_ref[...], cc_ref[...], preferred_element_type=F32)
            both = both[:, :L] + both[:, L:]
            pg_ref[pl.ds(pl.multiple_of(k * chunk, chunk), chunk), :] = both[:chunk] + both[chunk:]

        parts = [functools.partial(add_columns, pt_ref, k, slot_ref, acc_ref, n) for n in column_parts(acc_ref)]
        return [points_part] + parts

    sweep(rows // chunk, fill, use, (one_ref, two_ref))
    for c in range(nc):
        cs = cols_of(c)
        plan = direct_ref[:, cs] * q_ref[c : c + 1, :]
        cg_ref[cs, :] = ((acc_ref[:L, cs] + acc_ref[L:, cs]) + plan).T


MIB = 1024 * 1024
LIMIT = 15 * MIB


def call(kernel, name, buf, fetched, args, outs, scratch=(), keep=True):
    whole = pl.BlockSpec(memory_space=pltpu.VMEM)
    outside = pl.BlockSpec(memory_space=pltpu.HBM)
    shapes = [jax.ShapeDtypeStruct(o, F32) for o in outs]
    specs = [outside] * len(fetched) + [whole] * len(args)
    args = [pltpu.with_memory_space_constraint(a, pltpu.HBM) for a in fetched] + args
    scratch = [pltpu.VMEM(s, t) for s, t in scratch]
    if fetched:
        scratch += [pltpu.VMEM(a.shape, F32) for a in fetched] + [pltpu.SemaphoreType.DMA((len(fetched),))]
    aliases = {}
    if isinstance(buf, tuple):
        shapes = [pltpu.VMEM(buf, F32)] + shapes
    else:
        args = [pltpu.with_memory_space_constraint(buf, pltpu.VMEM)] + args
        specs = [whole] + specs
        if keep:
            shapes = [pltpu.VMEM(buf.shape, F32)] + shapes
            aliases = {0: 0}
    return pl.pallas_call(
        kernel,
        name=name,
        out_shape=shapes,
        in_specs=specs,
        out_specs=[whole] * len(shapes),
        scratch_shapes=scratch,
        input_output_aliases=aliases,
        compiler_params=pltpu.CompilerParams(vmem_limit_bytes=LIMIT),
    )(*args)


def over(axis, value):
    return lax.all_to_all(value, axis, 0, 0, tiled=True)


def sizes():
    return lax.axis_size("pt"), lax.axis_size("ct")


def per_device(points, centroids, cotangent):
    rows, width = points.shape
    cols = centroids.shape[0]
    npt, nct = sizes()
    share = (rows * npt) / (cols * nct)
    ratio = (cols * nct) / (rows * npt)
    scale = 3.0 / math.sqrt(width)
    rvec, cvec = (rows // L, L), (cols // L, L)
    to_pt, to_ct = (npt,) + cvec, (nct,) + rvec
    tall = [((rows, 4 * L), BF16), ((cols, 4 * L), BF16)]
    strip = ((8, cols), F32)
    chunk = min(CHUNK, rows // 2)
    slot = ((2 * chunk, cols), BF16)
    doubles = ((rows // chunk, 2 * L, 2 * chunk), BF16)
    wide = ((2 * L, cols), F32)
    part = functools.partial

    extra = -(-7 // (cols // L)) * (cols // L)
    height = 2 * cols + 2 * L + -(-extra // 8) * 8
    buf, stat = call(
        part(scores_kernel, scale), "scores", (height, cols), [points, centroids], [],
        [to_ct], tall,
    )
    stat = over("ct", stat)
    buf, stat = call(
        cols_kernel, "cols", buf, [cotangent, centroids], [stat],
        [to_pt], [strip, strip] + tall,
    )
    stat = over("pt", stat)
    buf, sums = call(plan_kernel, "plan", buf, [], [stat], [to_ct], [(cvec, F32), (rvec, F32)])
    sums = over("ct", sums)
    buf, stat = call(edges_kernel, "edges", buf, [], [sums], [(npt, 2) + cvec], [strip, strip])
    stat = over("pt", stat)
    buf, sums = call(
        part(rowback_kernel, share, ratio, scale), "rowback", buf, [points, cotangent], [stat],
        [to_ct], [doubles, wide, slot, slot],
    )
    sums = over("ct", sums)
    buf, sums = call(colback_kernel, "colback", buf, [], [sums], [to_pt], [strip])
    sums = over("pt", sums)
    buf, sums = call(lastrow_kernel, "lastrow", buf, [], [sums], [to_ct])
    sums = over("ct", sums)
    pg, cg = call(
        part(final_kernel, scale), "final", buf, [centroids], [sums],
        [(rows, width), (cols, width)],
        [(rvec, F32), (rvec, F32), (rvec, F32), doubles, ((cols, 2 * L), BF16), wide, slot, slot],
        keep=False,
    )
    point_grad = gather_points(pg)
    cg = over("pt", cg.reshape(npt, cols // npt, width))
    cg = jnp.sum(cg, axis=0)
    cg = over("pt", jnp.broadcast_to(cg[None], (npt, cols // npt, width)))
    return (point_grad, cg.reshape(cols, width))


def gather_points(value):
    n = lax.axis_size("ct")
    me = lax.axis_index("ct")
    size = value.shape[0] // n
    total = lax.dynamic_slice_in_dim(value, me * size, size)
    for step in range(1, n):
        block = lax.dynamic_slice_in_dim(value, (me + step) % n * size, size)
        total = total + lax.ppermute(block, "ct", [(k, (k + step) % n) for k in range(n)])
    return total


def solution(mesh):
    return jax.shard_map(
        per_device,
        mesh=mesh,
        in_specs=(P("pt", None), P("ct", None), P("pt", None)),
        out_specs=(P(("pt", "ct"), None), P("ct", None)),
        check_vma=False,
    )
```

```python
import functools
import itertools
import math

import jax
import jax.numpy as jnp
from jax import lax
from jax.experimental import pallas as pl
from jax.experimental.pallas import tpu as pltpu
from jax.sharding import PartitionSpec as P

L = 128
F32 = jnp.float32
BF16 = jnp.bfloat16
ROW_UNROLL = 16
PLAN_UNROLL = 8
CHUNK = 256
GROUP = 2
PART = (512, 512)
WIDE = 256


def split(x):
    high = x.astype(BF16)
    return high, (x - high.astype(F32)).astype(BF16)


def spread(vec_ref, index):
    return jnp.broadcast_to(vec_ref[pl.ds(index, 1), :], (L, L)).T


def fold_rows(tile):
    return jnp.sum(tile.T, axis=0, keepdims=True)


def fold_sub(tile, op):
    return op(tile.reshape(L // 8, 8, L), axis=0)


def cols_of(c):
    return slice(c * L, (c + 1) * L)


def rows_of(r):
    if isinstance(r, int):
        return slice(r * L, (r + 1) * L)
    return pl.ds(pl.multiple_of(r * L, L), L)


def send(out_ref, lead, value):
    for n in range(out_ref.shape[0]):
        out_ref[(n,) + lead] = value


def copies(out_ref):
    for n in range(1, out_ref.shape[0]):
        out_ref[n] = out_ref[0]


LEFT, RIGHT = (0, 0, 1, 1), (0, 1, 0, 1)


def pack(value_ref, out_ref, order, scale):
    terms = split(value_ref[...] * scale)
    for k, term in enumerate(order):
        out_ref[:, cols_of(k)] = terms[term]


def parts_of(rows, cols):
    for r in range(0, rows, min(PART[0], rows)):
        for c in range(0, cols, min(PART[1], cols)):
            yield slice(r, r + min(PART[0], rows)), slice(c, c + min(PART[1], cols))


def tile(a_ref, b_ref, out_ref, rs, cs):
    out_ref[rs, cs] = lax.dot_general(
        a_ref[rs, :], b_ref[cs, :], (((1,), (1,)), ((), ())), preferred_element_type=F32
    )


def each_row(nr, body, unroll=ROW_UNROLL):
    if unroll >= nr:
        for r in range(nr):
            body(r)
        return

    def step(r, carry):
        body(r)
        return carry

    lax.fori_loop(0, nr, step, 0, unroll=min(unroll, nr))


def begin(pairs, sem):
    moves = [pltpu.make_async_copy(src, dst, sem.at[n]) for n, (src, dst) in enumerate(pairs)]
    for move in moves:
        move.start()
    return moves


def planes(buf_ref):
    size = buf_ref.shape[1]
    return tuple(
        buf_ref.at[pl.ds(start, height), :]
        for start, height in ((0, size), (size, size), (2 * size, L), (2 * size + L, L))
    )


F1, S, IB, Q, H, Y, D = range(7)


def vec(buf_ref, name):
    size = buf_ref.shape[1]
    place = name % (size // L)
    return buf_ref.at[pl.ds(2 * size + 2 * L + (name // (size // L)) * (size // L), size // L), cols_of(place)]


def scores_kernel(scale, p_hbm, c_hbm, buf_ref, stat_ref, a_ref, b_ref, p_ref, c_ref, sem):
    moves = begin(((p_hbm, p_ref), (c_hbm, c_ref)), sem)
    moves[0].wait()
    pack(p_ref, a_ref, LEFT, scale * math.log2(math.e))
    moves[1].wait()
    pack(c_ref, b_ref, RIGHT, 1.0)
    z_ref = planes(buf_ref)[0]
    rows, cols = z_ref.shape
    nc = cols // L
    chunk = min(PART[0], rows)

    def sweep_row(r):
        rs = slice(r * L, (r + 1) * L)
        top = z_ref[rs, cols_of(0)]
        for c in range(1, nc):
            top = jnp.maximum(top, z_ref[rs, cols_of(c)])
        peak = jnp.max(top.T, axis=0, keepdims=True)
        wide = jnp.broadcast_to(peak, (L, L)).T
        total = jnp.zeros((L, L), F32)
        for c in range(nc):
            total = total + jnp.exp2(z_ref[rs, cols_of(c)] - wide)
        stat_ref[0, r : r + 1, :] = peak + jnp.log2(fold_rows(total))

    products = list(parts_of(rows, cols))
    each = len(products) * chunk // rows
    for rs, cs in products[:each]:
        tile(a_ref, b_ref, z_ref, rs, cs)
    for n in range(rows // chunk):
        coming = products[(n + 1) * each : (n + 2) * each]
        here = range(n * chunk // L, (n + 1) * chunk // L)
        done = 0
        for m, r in enumerate(here):
            until = len(coming) * (m + 1) // len(here)
            for rs, cs in coming[done:until]:
                tile(a_ref, b_ref, z_ref, rs, cs)
            done = until
            sweep_row(r)
    copies(stat_ref)


def merged(lse_ref):
    peak = lse_ref[0]
    for n in range(1, lse_ref.shape[0]):
        peak = jnp.maximum(peak, lse_ref[n])
    total = jnp.zeros_like(peak)
    for n in range(lse_ref.shape[0]):
        total = total + jnp.exp2(lse_ref[n] - peak)
    return peak + jnp.log2(total)


def summed(ref, *lead):
    total = ref[(0,) + lead]
    for n in range(1, ref.shape[0]):
        total = total + ref[(n,) + lead]
    return total


def cols_kernel(
    old_ref, cot_hbm, c_hbm, rowstat_ref, buf_ref, stat_ref, peak_ref, total_ref, left_ref, right_ref,
    cot_ref, c_ref, sem
):
    moves = begin(((cot_hbm, cot_ref), (c_hbm, c_ref)), sem)
    b_ref = planes(old_ref)[0]
    w_ref = planes(buf_ref)[1]
    rows, cols = b_ref.shape
    nc = cols // L
    f1_ref = vec(buf_ref, F1)
    f1_ref[...] = -merged(rowstat_ref)
    peak_ref[...] = jnp.full_like(peak_ref, -jnp.inf)
    total_ref[...] = jnp.zeros_like(total_ref)

    def sweep_row(r):
        rs = slice(r * L, (r + 1) * L)
        shift = spread(f1_ref, r)
        for c in range(nc):
            cs = cols_of(c)
            shifted = b_ref[rs, cs] + shift
            old = peak_ref[:, cs]
            new = jnp.maximum(old, fold_sub(shifted, jnp.max))
            terms = jnp.exp2(shifted.reshape(L // 8, 8, L) - new[None])
            total_ref[:, cs] = total_ref[:, cs] * jnp.exp2(old - new) + jnp.sum(terms, axis=0)
            peak_ref[:, cs] = new

    nr = rows // L
    early = nr // 2
    for r in range(early):
        sweep_row(r)
    for move in moves:
        move.wait()
    pack(cot_ref, left_ref, LEFT, 1.0)
    pack(c_ref, right_ref, RIGHT, 1.0)
    products = list(parts_of(rows, cols))
    done = 0
    for n, r in enumerate(range(early, nr)):
        until = len(products) * (n + 1) // (nr - early)
        for rs, cs in products[done:until]:
            tile(left_ref, right_ref, w_ref, rs, cs)
        done = until
        sweep_row(r)
    for c in range(nc):
        cs = cols_of(c)
        peak = jnp.max(peak_ref[:, cs], axis=0, keepdims=True)
        total = jnp.sum(total_ref[:, cs] * jnp.exp2(peak_ref[:, cs] - peak), axis=0, keepdims=True)
        stat_ref[0, c : c + 1, :] = peak + jnp.log2(total)
    copies(stat_ref)


def plan_kernel(old_ref, colstat_ref, buf_ref, sum_ref, shift_ref, f1_ref):
    z_ref, out_ref = planes(old_ref)[0], planes(buf_ref)[0]
    nr, nc = z_ref.shape[0] // L, z_ref.shape[1] // L
    s_ref = vec(buf_ref, S)
    f1_ref[...] = vec(old_ref, F1)[...]
    lse = merged(colstat_ref)
    shift_ref[...] = -lse
    s_ref[...] = jnp.exp2(lse)

    def body(r):
        shift = spread(f1_ref, r)
        waiting, totals = None, []
        for strip in range(0, L, 8):
            rs = pl.ds(pl.multiple_of(r * L + strip, 8), 8)
            row = shift[strip : strip + 8]
            values = [
                jnp.exp2((z_ref[rs, cols_of(c)] + row) + shift_ref[c : c + 1, :]) for c in range(nc)
            ]
            totals.append(functools.reduce(jnp.add, values))
            put(out_ref, waiting)
            waiting = (rs, values)
        put(out_ref, waiting)
        sum_ref[0, pl.ds(r, 1), :] = fold_rows(jnp.concatenate(totals))

    each_row(nr, body, PLAN_UNROLL)
    copies(sum_ref)


def put(out_ref, waiting):
    if waiting is not None:
        for c, value in enumerate(waiting[1]):
            out_ref[waiting[0], cols_of(c)] = value


def edges_kernel(old_ref, rowsum_ref, buf_ref, stat_ref, one_ref, two_ref):
    b_ref, w_ref = planes(old_ref)[:2]
    nr, nc = b_ref.shape[0] // L, b_ref.shape[1] // L
    ib_ref = vec(buf_ref, IB)
    ib_ref[...] = 1.0 / summed(rowsum_ref)
    one_ref[...] = jnp.zeros_like(one_ref)
    two_ref[...] = jnp.zeros_like(two_ref)

    def body(r):
        rs = rows_of(r)
        inv = spread(ib_ref, r)
        for c in range(nc):
            cs = cols_of(c)
            value = b_ref[rs, cs] * inv
            one_ref[:, cs] += fold_sub(value, jnp.sum)
            two_ref[:, cs] += fold_sub(value * w_ref[rs, cs], jnp.sum)

    each_row(nr, body)
    for c in range(nc):
        cs = cols_of(c)
        stat_ref[0, 0, c : c + 1, :] = jnp.sum(one_ref[:, cs], axis=0, keepdims=True)
        stat_ref[0, 1, c : c + 1, :] = jnp.sum(two_ref[:, cs], axis=0, keepdims=True)
    copies(stat_ref)


def double(out_ref, r, value):
    high, low = split(value)
    chunk = out_ref.shape[2] // 2
    k, place = divmod(r * L, chunk)
    out_ref[k, :L, place : place + L] = high
    out_ref[k, L:, place : place + L] = low
    out_ref[k, :L, chunk + place : chunk + place + L] = high


def sweep(count, fill, use, slots):
    def both(filling, using):
        for one, other in itertools.zip_longest(filling, using):
            if one is not None:
                one()
            if other is not None:
                other()

    def body(j, carry):
        k = 2 * j
        both(fill(k + 1, slots[1]), use(k, slots[0]))
        both(fill(k + 2, slots[0]), use(k + 1, slots[1]))
        return carry

    both(fill(0, slots[0]), [])
    lax.fori_loop(0, count // 2 - 1, body, 0)
    both(fill(count - 1, slots[1]), use(count - 2, slots[0]))
    for other in use(count - 1, slots[1]):
        other()


def pieces(piece, count, nc):
    groups = [range(c, min(c + GROUP, nc)) for c in range(0, nc, GROUP)]
    return [functools.partial(piece, sub, group) for sub in range(count) for group in groups]


def add_columns(left_ref, k, slot_ref, acc_ref, n):
    width = min(WIDE, acc_ref.shape[1])
    ns = slice(n * width, (n + 1) * width)
    chunk = slot_ref.shape[0] // 2
    acc_ref[:, ns] += jnp.dot(left_ref[k, :, :chunk], slot_ref[:chunk, ns], preferred_element_type=F32)
    acc_ref[:L, ns] += jnp.dot(left_ref[k, :L, chunk:], slot_ref[chunk:, ns], preferred_element_type=F32)


def column_parts(acc_ref):
    return range(acc_ref.shape[1] // min(WIDE, acc_ref.shape[1]))


def rowback_kernel(
    share, ratio, scale, old_ref, p_hbm, cot_hbm, colsum_ref, buf_ref, sum_ref,
    ct_ref, acc_ref, one_ref, two_ref, p_ref, cot_ref, sem
):
    moves = begin(((p_hbm, p_ref), (cot_hbm, cot_ref)), sem)
    b_ref, w_ref = planes(old_ref)[:2]
    pt_ref, direct_ref = planes(buf_ref)[2:]
    rows, cols = b_ref.shape
    nr, nc = rows // L, cols // L
    ib_ref, q_ref, h_ref = vec(old_ref, IB), vec(buf_ref, Q), vec(buf_ref, H)
    q = share / summed(colsum_ref, 0)
    q_ref[...] = q
    h_ref[...] = ratio * (q * summed(colsum_ref, 1))
    acc_ref[...] = jnp.zeros_like(acc_ref)

    def body(r):
        rs = rows_of(r)
        total = jnp.zeros((L, L), F32)
        for c in range(nc):
            cs = cols_of(c)
            total = total + (b_ref[rs, cs] * q_ref[c : c + 1, :]) * (w_ref[rs, cs] - h_ref[c : c + 1, :])
        sum_ref[0, pl.ds(r, 1), :] = fold_rows(total)

    each_row(nr, body)
    for move in moves:
        move.wait()
    for r in range(nr):
        rs = slice(r * L, (r + 1) * L)
        pt_ref[:, rs] = (p_ref[rs, :] * scale).T
        double(ct_ref, r, cot_ref[rs, :].T * ib_ref[r : r + 1, :])
    chunk = one_ref.shape[0] // 2

    def fill(k, slot_ref):
        def piece(sub, group):
            rs = rows_of(k * (chunk // L) + sub)
            for c in group:
                high, low = split(b_ref[rs, cols_of(c)])
                slot_ref[sub * L : (sub + 1) * L, cols_of(c)] = high
                slot_ref[chunk + sub * L : chunk + (sub + 1) * L, cols_of(c)] = low

        return pieces(piece, chunk // L, nc)

    def use(k, slot_ref):
        return [functools.partial(add_columns, ct_ref, k, slot_ref, acc_ref, n) for n in column_parts(acc_ref)]

    sweep(rows // chunk, fill, use, (one_ref, two_ref))
    direct_ref[...] = acc_ref[:L, :] + acc_ref[L:, :]
    copies(sum_ref)


def colback_kernel(old_ref, rowsum_ref, buf_ref, sum_ref, acc_ref):
    b_ref = planes(old_ref)[0]
    nr, nc = b_ref.shape[0] // L, b_ref.shape[1] // L
    ib_ref, y_ref = vec(old_ref, IB), vec(buf_ref, Y)
    y_ref[...] = (summed(rowsum_ref) * ib_ref[...]) * ib_ref[...]
    acc_ref[...] = jnp.zeros_like(acc_ref)

    def body(r):
        rs = rows_of(r)
        y = spread(y_ref, r)
        for c in range(nc):
            cs = cols_of(c)
            acc_ref[:, cs] += fold_sub(b_ref[rs, cs] * y, jnp.sum)

    each_row(nr, body)
    for c in range(nc):
        sum_ref[0, c : c + 1, :] = -jnp.sum(acc_ref[:, cols_of(c)], axis=0, keepdims=True)
    copies(sum_ref)


def lastrow_kernel(old_ref, colsum_ref, buf_ref, sum_ref):
    b_ref = planes(old_ref)[0]
    nr, nc = b_ref.shape[0] // L, b_ref.shape[1] // L
    d_ref = vec(buf_ref, D)
    d_ref[...] = summed(colsum_ref)

    def body(r):
        rs = rows_of(r)
        total = jnp.zeros((L, L), F32)
        for c in range(nc):
            total = total + b_ref[rs, cols_of(c)] * d_ref[c : c + 1, :]
        sum_ref[0, pl.ds(r, 1), :] = -fold_rows(total)

    each_row(nr, body)
    copies(sum_ref)


def final_kernel(
    scale, old_ref, c_hbm, rowsum_ref, pg_ref, cg_ref,
    ib_ref, y_ref, f_ref, pt_ref, cc_ref, acc_ref, one_ref, two_ref, c_ref, sem
):
    moves = begin(((c_hbm, c_ref),), sem)
    b_ref, w_ref, p_ref, direct_ref = planes(old_ref)
    rows, cols = b_ref.shape
    nr, nc = rows // L, cols // L
    s_ref, q_ref, h_ref, d_ref = (vec(old_ref, name) for name in (S, Q, H, D))
    f_ref[...] = summed(rowsum_ref)
    ib_ref[...] = vec(old_ref, IB)[...]
    y_ref[...] = vec(old_ref, Y)[...]
    acc_ref[...] = jnp.zeros_like(acc_ref)
    for r in range(nr):
        double(pt_ref, r, p_ref[:, r * L : (r + 1) * L])
    for move in moves:
        move.wait()
    high, low = split(c_ref[...] * scale)
    cc_ref[:, :L] = high
    cc_ref[:, L:] = low
    chunk = one_ref.shape[0] // 2

    def fill(k, slot_ref):
        def piece(sub, group):
            r = k * (chunk // L) + sub
            rs = rows_of(r)
            inv, y, f = spread(ib_ref, r), spread(y_ref, r), spread(f_ref, r)
            for c in group:
                row, cs = slice(c, c + 1), cols_of(c)
                plan = (q_ref[row, :] * inv) * (w_ref[rs, cs] - h_ref[row, :])
                factor = (y + d_ref[row, :]) + s_ref[row, :] * f
                high, low = split(b_ref[rs, cs] * (plan - factor))
                slot_ref[sub * L : (sub + 1) * L, cs] = high
                slot_ref[chunk + sub * L : chunk + (sub + 1) * L, cs] = low

        return pieces(piece, chunk // L, nc)

    def use(k, slot_ref):
        def points_part():
            both = jnp.dot(slot_ref[...], cc_ref[...], preferred_element_type=F32)
            both = both[:, :L] + both[:, L:]
            pg_ref[pl.ds(pl.multiple_of(k * chunk, chunk), chunk), :] = both[:chunk] + both[chunk:]

        parts = [functools.partial(add_columns, pt_ref, k, slot_ref, acc_ref, n) for n in column_parts(acc_ref)]
        return parts + [points_part]

    sweep(rows // chunk, fill, use, (one_ref, two_ref))
    for c in range(nc):
        cs = cols_of(c)
        plan = direct_ref[:, cs] * q_ref[c : c + 1, :]
        cg_ref[cs, :] = ((acc_ref[:L, cs] + acc_ref[L:, cs]) + plan).T


MIB = 1024 * 1024
LIMIT = 15 * MIB


def call(kernel, name, buf, fetched, args, outs, scratch=(), keep=True):
    whole = pl.BlockSpec(memory_space=pltpu.VMEM)
    outside = pl.BlockSpec(memory_space=pltpu.HBM)
    shapes = [jax.ShapeDtypeStruct(o, F32) for o in outs]
    specs = [outside] * len(fetched) + [whole] * len(args)
    args = [pltpu.with_memory_space_constraint(a, pltpu.HBM) for a in fetched] + args
    scratch = [pltpu.VMEM(s, t) for s, t in scratch]
    if fetched:
        scratch += [pltpu.VMEM(a.shape, F32) for a in fetched] + [pltpu.SemaphoreType.DMA((len(fetched),))]
    aliases = {}
    if isinstance(buf, tuple):
        shapes = [pltpu.VMEM(buf, F32)] + shapes
    else:
        args = [pltpu.with_memory_space_constraint(buf, pltpu.VMEM)] + args
        specs = [whole] + specs
        if keep:
            shapes = [pltpu.VMEM(buf.shape, F32)] + shapes
            aliases = {0: 0}
    return pl.pallas_call(
        kernel,
        name=name,
        out_shape=shapes,
        in_specs=specs,
        out_specs=[whole] * len(shapes),
        scratch_shapes=scratch,
        input_output_aliases=aliases,
        compiler_params=pltpu.CompilerParams(vmem_limit_bytes=LIMIT),
    )(*args)


def over(axis, value):
    return lax.all_to_all(value, axis, 0, 0, tiled=True)


def sizes():
    return lax.axis_size("pt"), lax.axis_size("ct")


def per_device(points, centroids, cotangent):
    rows, width = points.shape
    cols = centroids.shape[0]
    npt, nct = sizes()
    share = (rows * npt) / (cols * nct)
    ratio = (cols * nct) / (rows * npt)
    scale = 3.0 / math.sqrt(width)
    rvec, cvec = (rows // L, L), (cols // L, L)
    to_pt, to_ct = (npt,) + cvec, (nct,) + rvec
    tall = [((rows, 4 * L), BF16), ((cols, 4 * L), BF16)]
    strip = ((8, cols), F32)
    chunk = min(CHUNK, rows // 2)
    slot = ((2 * chunk, cols), BF16)
    doubles = ((rows // chunk, 2 * L, 2 * chunk), BF16)
    wide = ((2 * L, cols), F32)
    part = functools.partial

    extra = -(-7 // (cols // L)) * (cols // L)
    height = 2 * cols + 2 * L + -(-extra // 8) * 8
    buf, stat = call(
        part(scores_kernel, scale), "scores", (height, cols), [points, centroids], [],
        [to_ct], tall,
    )
    stat = over("ct", stat)
    buf, stat = call(
        cols_kernel, "cols", buf, [cotangent, centroids], [stat],
        [to_pt], [strip, strip] + tall,
    )
    stat = over("pt", stat)
    buf, sums = call(plan_kernel, "plan", buf, [], [stat], [to_ct], [(cvec, F32), (rvec, F32)])
    sums = over("ct", sums)
    buf, stat = call(edges_kernel, "edges", buf, [], [sums], [(npt, 2) + cvec], [strip, strip])
    stat = over("pt", stat)
    buf, sums = call(
        part(rowback_kernel, share, ratio, scale), "rowback", buf, [points, cotangent], [stat],
        [to_ct], [doubles, wide, slot, slot],
    )
    sums = over("ct", sums)
    buf, sums = call(colback_kernel, "colback", buf, [], [sums], [to_pt], [strip])
    sums = over("pt", sums)
    buf, sums = call(lastrow_kernel, "lastrow", buf, [], [sums], [to_ct])
    sums = over("ct", sums)
    pg, cg = call(
        part(final_kernel, scale), "final", buf, [centroids], [sums],
        [(rows, width), (cols, width)],
        [(rvec, F32), (rvec, F32), (rvec, F32), doubles, ((cols, 2 * L), BF16), wide, slot, slot],
        keep=False,
    )
    point_grad = gather_points(pg)
    cg = over("pt", cg.reshape(npt, cols // npt, width))
    cg = jnp.sum(cg, axis=0)
    cg = over("pt", jnp.broadcast_to(cg[None], (npt, cols // npt, width)))
    return (point_grad, cg.reshape(cols, width))


def gather_points(value):
    n = lax.axis_size("ct")
    me = lax.axis_index("ct")
    size = value.shape[0] // n
    total = lax.dynamic_slice_in_dim(value, me * size, size)
    for step in range(1, n):
        block = lax.dynamic_slice_in_dim(value, (me + step) % n * size, size)
        total = total + lax.ppermute(block, "ct", [(k, (k + step) % n) for k in range(n)])
    return total


def solution(mesh):
    return jax.shard_map(
        per_device,
        mesh=mesh,
        in_specs=(P("pt", None), P("ct", None), P("pt", None)),
        out_specs=(P(("pt", "ct"), None), P("ct", None)),
        check_vma=False,
    )
```
